128 devices in a mesh: tile: 64 (over y, x, z), sec: 2 (over core).
Axes of the slice: x: 4, y: 4, z: 4, core: 2. Of those that a mesh axis runs over, the one named last changes fastest.
Arguments:
- features: bfloat16 [2, 2048, 384, 128], P('sec', 'tile'), may hold values from -6 to 6
- fold_mask: int32 [2, 2048, 384], P('sec', 'tile'), may hold values 0 or 1
- encoder_weight: bfloat16 [3, 3, 128, 128], replicated, may hold values from -0.1875 to 0.1875
- encoder_bias: float32 [128], replicated, may hold values from -3 to 3
- head_weight: bfloat16 [3, 3, 128, 256], replicated, may hold values from -0.1875 to 0.1875
- head_bias: float32 [256], replicated, may hold values from -3 to 3
- final_weight: bfloat16 [256, 256], replicated, may hold values from -0.375 to 0.375
- final_bias: float32 [256], replicated, may hold values from -3 to 3
- pair_source: int32 [2, 4096], P('sec', 'tile'), may hold values from 0 to 95
- pair_target: int32 [2, 4096], replicated, may hold values from 0 to 6143, as said below
Outputs:
- descriptors: bfloat16 [2, 2048, 384, 256], P('sec', 'tile')
- confidence: float32 [2, 4096, 128], P('sec', 'tile')
The draws below stay inside these ranges and needn't reach their ends.
Inputs may be any that keep to these rules, and one draw needn't show every extreme that they name: `pair_target`: row s names blocks of section 1 - s by their number in that section; the 64 entries of one band name at most 2 blocks of any one band of the other section, and exactly 2 of some band.
All inputs are finite; a program needn't handle non-finite values. No bound on the sum of `fold_mask` on one device may be relied on, other than what follows from the above.
Results may differ from the reference program's by a relative error of at most 0.0076.
Values may be sent and summed in bfloat16 or wider, within the bound.
No kernel may reach another device: no remote copies, remote signals or barrier semaphores. Data moves between devices by JAX's collectives and lax.ppermute only.
A program may use at most 128 MiB of HBM per device.

```python
import jax
import jax.numpy as jnp
from jax import lax

C_ENC = 128
C_DESC = 256
BLOCK = 128
CC = 384
PAIRS = 64
NR = 2048
NB = 96
TOTAL_BLOCKS = 6144
TOTAL_PAIRS = 4096
CAP = 2


def draw_pair_target(key, part):
    key = jax.random.fold_in(key, 7)
    tile_count = TOTAL_PAIRS // PAIRS
    row_keys = jax.random.split(key, 2 * tile_count)

    def one_row(row_key):
        first_key, order_key, block_key, shuffle_key = jax.random.split(row_key, 4)
        crowded = jax.random.randint(first_key, (), 0, tile_count)
        priority = jax.random.permutation(order_key, tile_count * CAP).astype(jnp.int32)
        slot_owner = jnp.arange(tile_count * CAP, dtype=jnp.int32) // CAP
        priority = jnp.where(slot_owner == crowded, -1, priority)
        chosen = jnp.argsort(priority, stable=True)[:PAIRS]
        chosen = chosen[jax.random.permutation(shuffle_key, PAIRS)]
        owners = (chosen // CAP).astype(jnp.int32)
        within = jax.random.randint(block_key, (PAIRS,), 0, NB)
        return owners * NB + within
    return jax.vmap(one_row)(row_keys).reshape(2, TOTAL_PAIRS).astype(jnp.int32)


def place_ends(values, rng, smallest, top_value):
    shape = values.shape
    spot = [jax.random.randint(jax.random.fold_in(rng, axis), (), 0, shape[axis]) for axis in range(len(shape))]
    values = values.at[tuple(spot)].set(smallest)
    longest = shape.index(max(shape))
    spot[longest] = (spot[longest] + 1) % shape[longest]
    return values.at[tuple(spot)].set(top_value)


def levels(rng, shape, pieces, low, high):
    def one(position, parts):
        draws = jax.random.uniform(jax.random.fold_in(jax.random.fold_in(rng, 6), position), (parts,), jnp.float32, low / len(pieces), high / len(pieces))
        return jnp.repeat(jnp.exp(draws), shape[position] // parts).reshape((-1,) + (1,) * (len(shape) - position - 1))

    factor_of = one(*pieces[0])
    for cut in pieces[1:]:
        factor_of = factor_of * one(*cut)
    return factor_of


def gaussian(stream_key, shape, deviation, bound, shards=(), held_as=jnp.bfloat16):
    drawn = jax.random.normal(stream_key, shape, jnp.float32) * deviation
    if len(shards) > 0:
        drawn = levels(stream_key, shape, shards, -0.22, 0.18) * drawn
    return jnp.clip(drawn, min=-bound, max=bound).astype(held_as)


def setup_inputs(seed: int = 0) -> dict:
    keys = jax.random.split(jax.random.key(seed), 11)
    return {
        "features": gaussian(keys[0], (2, NR, CC, C_ENC), 1.0, 6.0, ((0, 2), (1, 64))),
        "fold_mask": place_ends((jax.random.randint(keys[1], (2, NR, CC), 0, 8) < 1).astype(jnp.int32), jax.random.fold_in(keys[1], 1), 0, 1),
        "encoder_weight": gaussian(keys[2], (3, 3, C_ENC, C_ENC), (9 * C_ENC) ** -0.5, 0.1875),
        "encoder_bias": gaussian(keys[3], (C_ENC,), 0.5, 3.0, (), jnp.float32),
        "head_weight": gaussian(keys[4], (3, 3, C_ENC, C_DESC), (9 * C_ENC) ** -0.5, 0.1875),
        "head_bias": gaussian(keys[5], (C_DESC,), 0.5, 3.0, (), jnp.float32),
        "final_weight": gaussian(keys[6], (C_DESC, C_DESC), C_DESC ** -0.5, 0.375),
        "final_bias": gaussian(keys[7], (C_DESC,), 0.5, 3.0, (), jnp.float32),
        "pair_source": place_ends(jax.random.randint(keys[8], (2, TOTAL_PAIRS), 0, NB), jax.random.fold_in(keys[8], 1), 0, NB - 1).astype(jnp.int32),
        "pair_target": draw_pair_target(jax.random.fold_in(keys[10], 71), 0),
    }


SCORE_SCALE = 10.0
FOLD_PENALTY = 200.0

def convolve(source, kernel):
    result = lax.conv_general_dilated(source.astype(jnp.float32)[None], kernel.astype(jnp.float32), (1, 1), ((1, 1), (1, 1)), dimension_numbers=('NHWC', 'HWIO', 'NHWC'), precision=lax.Precision.HIGHEST)
    return result[0]

def dual_score(scores):
    row_peak = lax.optimization_barrier(jnp.max(scores, axis=-1, keepdims=True))
    row_weight = jnp.exp(scores - row_peak)
    row_soft = row_weight / lax.optimization_barrier(jnp.sum(row_weight, axis=-1, keepdims=True))
    column_peak = lax.optimization_barrier(jnp.max(scores, axis=-2, keepdims=True))
    column_weight = jnp.exp(scores - column_peak)
    column_soft = column_weight / lax.optimization_barrier(jnp.sum(column_weight, axis=-2, keepdims=True))
    return lax.optimization_barrier(jnp.max(row_soft * column_soft, axis=-1))

def reference(features, fold_mask, encoder_weight, encoder_bias, head_weight, head_bias, final_weight, final_bias, pair_source, pair_target):
    described_all = []
    for section in range(2):
        encoded = jax.nn.relu(convolve(features[section], encoder_weight) + encoder_bias).astype(jnp.bfloat16)
        hidden = jax.nn.relu(convolve(encoded, head_weight) + head_bias).astype(jnp.bfloat16)
        raw_output = jnp.dot(hidden.reshape(-1, C_DESC), final_weight, preferred_element_type=jnp.float32) + final_bias
        described = raw_output / jnp.sqrt(lax.optimization_barrier(jnp.sum(raw_output * raw_output, axis=-1, keepdims=True)) + 1e-06)
        described_all.append(described.astype(jnp.bfloat16).reshape(NR, CC, C_DESC))
    descriptors = jnp.stack(described_all)
    blocks = descriptors.reshape(2, TOTAL_BLOCKS, BLOCK, C_DESC)
    folds = fold_mask.reshape(2, TOTAL_BLOCKS, BLOCK).astype(jnp.float32)
    band_start = jnp.arange(TOTAL_PAIRS, dtype=jnp.int32) // PAIRS * NB
    results = []
    for section in range(2):
        anchor_index = band_start + pair_source[section]
        partner_index = pair_target[section]
        anchor = blocks[section][anchor_index].astype(jnp.float32)
        partner = blocks[1 - section][partner_index].astype(jnp.float32)
        products = jnp.einsum('pid,pjd->pij', anchor, partner, precision=lax.Precision.HIGHEST)
        penalty = folds[section][anchor_index][:, :, None] + folds[1 - section][partner_index][:, None, :]
        scores = SCORE_SCALE * products - FOLD_PENALTY * penalty
        results.append(dual_score(scores))
    return (descriptors, jnp.stack(results))
```

```python
import functools

import jax
import jax.numpy as jnp
from jax import lax
from jax.experimental import pallas as pl
from jax.experimental.pallas import tpu as pltpu
from jax.sharding import PartitionSpec as P

BLOCK = 128
SCORE_SCALE = 10.0
FOLD_PENALTY = 200.0
ROWS_STEP = 4
PAIRS_STEP = 8


def side_copies(rows):
    cols = rows.shape[1]
    flat = rows.reshape(rows.shape[0] * cols, rows.shape[2])
    column = lax.broadcasted_iota(jnp.int32, rows.shape, 1).reshape(flat.shape)
    before = jnp.where(column == 0, 0.0, pltpu.roll(flat, 1, 0))
    after = jnp.where(column == cols - 1, 0.0, pltpu.roll(flat, flat.shape[0] - 1, 0))
    return [v.reshape(rows.shape).astype(jnp.bfloat16) for v in (before, flat, after)]


def describe_kernel(
    edge_ref, low_ref, own_ref, high_ref, enc_w_ref, enc_b_ref, head_w_ref, head_b_ref,
    final_w_ref, final_b_ref, out_ref, wide_ref, enc_ref, pair_w_ref,
):
    step = pl.program_id(0)
    last = pl.num_programs(0) - 1
    chan = own_ref.shape[2]

    def put_features(first, rows):
        for b, copy in enumerate(side_copies(rows.astype(jnp.float32))):
            wide_ref[pl.ds(first, 2), :, b * chan : (b + 1) * chan] = copy

    def encode(first):
        window = jnp.concatenate([wide_ref[first + a] for a in range(4)], axis=-1)
        both = jnp.dot(window, pair_w_ref[...], preferred_element_type=jnp.float32)
        both = jnp.maximum(both + enc_b_ref[...], 0.0)
        keep = [
            jnp.logical_not((first + d == edge_ref[0]) | (first + d == edge_ref[1]))
            for d in range(2)
        ]
        rows = jnp.stack(
            [jnp.where(keep[d], both[:, d * chan : (d + 1) * chan], 0.0) for d in range(2)]
        )
        for b, copy in enumerate(side_copies(rows)):
            enc_ref[pl.ds(first, 2), :, b * chan : (b + 1) * chan] = copy

    @pl.when(step == 0)
    def _():
        for p in range(4):
            for b in range(3):
                k = pl.ds((p * 3 + b) * chan, chan)
                zero = jnp.zeros((chan, chan), jnp.bfloat16)
                pair_w_ref[k, 0:chan] = enc_w_ref[p, b] if p < 3 else zero
                pair_w_ref[k, chan : 2 * chan] = enc_w_ref[p - 1, b] if p > 0 else zero
        put_features(0, low_ref[...])
        put_features(2, own_ref[pl.ds(0, 2)])
        encode(0)

    base = step * ROWS_STEP
    put_features(base + 4, own_ref[pl.ds(base + 2, 2)])

    @pl.when(step < last)
    def _():
        put_features(base + 6, own_ref[pl.ds(base + 4, 2)])

    @pl.when(step == last)
    def _():
        put_features(base + 6, high_ref[...])

    encode(base + 2)
    encode(base + 4)
    for r in range(0, ROWS_STEP, 2):
        parts = [enc_ref[pl.ds(base + r + a, 2)] for a in range(3)]
        cols = parts[0].shape[1]
        window = jnp.concatenate([v.reshape(2 * cols, 3 * chan) for v in parts], axis=-1)
        hidden = jnp.dot(window, head_w_ref[...], preferred_element_type=jnp.float32)
        hidden = jnp.maximum(hidden + head_b_ref[...], 0.0).astype(jnp.bfloat16)
        raw = jnp.dot(hidden, final_w_ref[...], preferred_element_type=jnp.float32)
        raw = raw + final_b_ref[...]
        norm = jnp.sum(raw * raw, axis=-1, keepdims=True)
        unit = (raw * lax.rsqrt(norm + 1e-06)).astype(jnp.bfloat16)
        out_ref[pl.ds(r, 2)] = unit.reshape(2, cols, unit.shape[1])


def describe(edge, low, own, high, enc_w, enc_b, head_w, head_b, final_w, final_b):
    rows, cols, chan = own.shape
    desc = final_w.shape[1]
    whole = pl.BlockSpec(memory_space=pltpu.VMEM)
    macs = rows * cols * (12 * chan * chan + 9 * chan * desc + desc * desc)
    return pl.pallas_call(
        describe_kernel,
        grid=(rows // ROWS_STEP,),
        in_specs=[pl.BlockSpec(memory_space=pltpu.SMEM)] + [whole] * 9,
        out_specs=pl.BlockSpec((ROWS_STEP, cols, desc), lambda i: (i, 0, 0)),
        out_shape=jax.ShapeDtypeStruct((rows, cols, desc), jnp.bfloat16),
        scratch_shapes=[
            pltpu.VMEM((rows + 4, cols, 3 * chan), jnp.bfloat16),
            pltpu.VMEM((rows + 2, cols, 3 * chan), jnp.bfloat16),
            pltpu.VMEM((12 * chan, 2 * chan), jnp.bfloat16),
        ],
        compiler_params=pltpu.CompilerParams(vmem_limit_bytes=56 * 2**20),
        cost_estimate=pl.CostEstimate(
            flops=2 * macs, bytes_accessed=rows * cols * (chan + desc) * 2, transcendentals=rows * cols
        ),
    )(
        edge, low, own, high, enc_w, jnp.tile(enc_b, 2)[None], head_w.reshape(-1, desc),
        head_b[None], final_w, final_b[None],
    )


def match_kernel(source_ref, slot_ref, anchor_fold_ref, partner_fold_ref, *refs):
    anchors, partners, out_ref = refs[:PAIRS_STEP], refs[PAIRS_STEP : 2 * PAIRS_STEP], refs[-1]
    first = pl.program_id(0) * PAIRS_STEP
    folds = jnp.concatenate(
        [partner_fold_ref[pl.ds(slot_ref[first + n], 1)] for n in range(PAIRS_STEP)]
    )
    folds = jnp.transpose(folds)
    for n in range(PAIRS_STEP):
        products = lax.dot_general(
            partners[n][0], anchors[n][0], (((1,), (1,)), ((), ())),
            preferred_element_type=jnp.float32,
        )
        penalty = anchor_fold_ref[pl.ds(source_ref[first + n], 1)] + folds[:, n : n + 1]
        scores = SCORE_SCALE * products - FOLD_PENALTY * penalty
        over_j = jnp.exp(scores - jnp.max(scores, axis=0, keepdims=True))
        over_i = jnp.exp(scores - jnp.max(scores, axis=1, keepdims=True))
        sum_j = jnp.sum(over_j, axis=0, keepdims=True)
        sum_i = jnp.sum(over_i, axis=1, keepdims=True)
        best = jnp.max(over_j * (over_i * (1.0 / sum_i)), axis=0, keepdims=True)
        out_ref[n : n + 1, :] = best / sum_j


def match(source, slot, anchor_folds, partner_folds, blocks, arrived):
    pairs = source.shape[0]
    shape = (1,) + blocks.shape[1:]

    def spec(which, n):
        return pl.BlockSpec(shape, lambda i, s, t: ((s, t)[which][i * PAIRS_STEP + n], 0, 0))

    return pl.pallas_call(
        match_kernel,
        grid_spec=pltpu.PrefetchScalarGridSpec(
            num_scalar_prefetch=2,
            grid=(pairs // PAIRS_STEP,),
            in_specs=[pl.BlockSpec(memory_space=pltpu.VMEM)] * 2
            + [spec(0, n) for n in range(PAIRS_STEP)]
            + [spec(1, n) for n in range(PAIRS_STEP)],
            out_specs=pl.BlockSpec((PAIRS_STEP, BLOCK), lambda i, s, t: (i, 0)),
        ),
        out_shape=jax.ShapeDtypeStruct((pairs, BLOCK), jnp.float32),
        compiler_params=pltpu.CompilerParams(vmem_limit_bytes=32 * 2**20),
    )(
        source, slot, anchor_folds, partner_folds,
        *([blocks] * PAIRS_STEP), *([arrived] * PAIRS_STEP),
    )


def pick_kernel(chosen_ref, blocks_ref, out_ref, sem):
    count = out_ref.shape[0]

    def copy(n):
        return pltpu.make_async_copy(blocks_ref.at[chosen_ref[n]], out_ref.at[n], sem)

    pl.loop(0, count)(lambda n: copy(n).start())
    pltpu.make_async_copy(out_ref, out_ref, sem).wait()


def pick(chosen, blocks):
    count = chosen.shape[0]
    return pl.pallas_call(
        pick_kernel,
        in_specs=[pl.BlockSpec(memory_space=pltpu.SMEM), pl.BlockSpec(memory_space=pl.ANY)],
        out_specs=pl.BlockSpec(memory_space=pl.ANY),
        out_shape=jax.ShapeDtypeStruct((count,) + blocks.shape[1:], blocks.dtype),
        scratch_shapes=[pltpu.SemaphoreType.DMA],
    )(chosen, blocks)


def local(
    features, fold_mask, encoder_weight, encoder_bias, head_weight, head_bias,
    final_weight, final_bias, pair_source, pair_target,
):
    own_band = features[0]
    band_rows, band_cols, _ = own_band.shape
    tile_count = lax.axis_size("tile")
    tile_here = lax.axis_index("tile")
    section = lax.axis_index("sec")
    down = [(i, i + 1) for i in range(tile_count - 1)]
    up = [(j, i) for i, j in down]
    low = lax.ppermute(own_band[-2:], "tile", down)
    high = lax.ppermute(own_band[:2], "tile", up)
    edge = jnp.stack(
        [
            jnp.where(tile_here == 0, 0, -1),
            jnp.where(tile_here == tile_count - 1, band_rows + 1, -1),
        ]
    ).astype(jnp.int32)
    described = describe(
        edge, low, own_band, high, encoder_weight, encoder_bias, head_weight, head_bias,
        final_weight, final_bias,
    )
    desc = described.shape[2]
    block_count = band_rows * band_cols // BLOCK
    own_blocks = described.reshape(block_count, BLOCK, desc)
    own_folds = fold_mask[0].reshape(block_count, BLOCK).astype(jnp.bfloat16)
    pair_count = pair_source.shape[1]
    capacity = max(2, 2 * pair_count // tile_count)
    wanted_by_others = lax.dynamic_index_in_dim(
        pair_target, 1 - section, 0, keepdims=False
    ).reshape(tile_count, pair_count)
    matched = (wanted_by_others // block_count == tile_here).astype(jnp.int32)
    order_rank = jnp.cumsum(matched, axis=1) - matched
    slot_hot = matched[:, :, None] * (
        order_rank[:, :, None] == jnp.arange(capacity)[None, None, :]
    ).astype(jnp.int32)
    chosen = jnp.sum(slot_hot * (wanted_by_others % block_count)[:, :, None], axis=1)
    send_folds = own_folds[chosen]
    send_blocks = pick(chosen.reshape(-1), own_blocks).reshape(
        tile_count, capacity, BLOCK, desc
    )
    swap = [(0, 1), (1, 0)]
    arrived_folds = lax.ppermute(
        lax.all_to_all(send_folds, "tile", split_axis=0, concat_axis=0, tiled=True), "sec", swap
    )
    arrived_blocks = lax.ppermute(
        lax.all_to_all(send_blocks, "tile", split_axis=0, concat_axis=0, tiled=True), "sec", swap
    )
    own_targets = lax.dynamic_index_in_dim(pair_target, section, 0, keepdims=False).reshape(
        tile_count, pair_count
    )
    own_targets = lax.dynamic_index_in_dim(own_targets, tile_here, 0, keepdims=False)
    owners = own_targets // block_count
    earlier = jnp.arange(pair_count)[None, :] < jnp.arange(pair_count)[:, None]
    slot_rank = jnp.sum(((owners[None, :] == owners[:, None]) & earlier).astype(jnp.int32), axis=1)
    slot_index = owners * capacity + slot_rank
    confidence = match(
        pair_source[0],
        slot_index,
        fold_mask[0].reshape(block_count, BLOCK).astype(jnp.float32),
        arrived_folds.reshape(tile_count * capacity, BLOCK).astype(jnp.float32),
        own_blocks,
        arrived_blocks.reshape(tile_count * capacity, BLOCK, desc),
    )
    return (described.reshape(1, band_rows, band_cols, desc), confidence[None])


def solution(mesh):
    return jax.shard_map(
        local,
        mesh=mesh,
        in_specs=(
            P("sec", "tile", None, None), P("sec", "tile", None), P(), P(), P(), P(), P(), P(),
            P("sec", "tile"), P(),
        ),
        out_specs=(P("sec", "tile", None, None), P("sec", "tile", None)),
        check_vma=False,
    )
```

```python
import functools

import jax
import jax.numpy as jnp
from jax import lax
from jax.experimental import pallas as pl
from jax.experimental.pallas import tpu as pltpu
from jax.sharding import PartitionSpec as P

BLOCK = 128
SCORE_SCALE = 10.0
FOLD_PENALTY = 200.0
ROWS_STEP = 4
PAIRS_STEP = 8


def side_copies(rows):
    cols = rows.shape[1]
    flat = rows.reshape(rows.shape[0] * cols, rows.shape[2])
    column = lax.broadcasted_iota(jnp.int32, rows.shape, 1).reshape(flat.shape)
    before = jnp.where(column == 0, 0.0, pltpu.roll(flat, 1, 0))
    after = jnp.where(column == cols - 1, 0.0, pltpu.roll(flat, flat.shape[0] - 1, 0))
    return [v.reshape(rows.shape).astype(jnp.bfloat16) for v in (before, flat, after)]


def describe_kernel(
    chosen_ref, source_ref, low_ref, own_ref, high_ref, enc_w_ref, enc_b_ref, head_w_ref,
    head_b_ref, final_w_ref, final_b_ref, out_ref, send_ref, anchor_ref, wide_ref, enc_ref,
    pair_w_ref, all_ref, out_sem, send_sem, anchor_sem,
):
    step = pl.program_id(0)
    last = pl.num_programs(0) - 1
    chan = own_ref.shape[2]
    tile_here = lax.axis_index("tile")
    top = jnp.where(tile_here == 0, 0, -1)
    bottom = jnp.where(tile_here == lax.axis_size("tile") - 1, enc_ref.shape[0] - 1, -1)
    enc_b = jnp.concatenate([enc_b_ref[...]] * 2, axis=-1)

    def put_features(first, rows):
        for b, copy in enumerate(side_copies(rows.astype(jnp.float32))):
            wide_ref[pl.ds(first, 2), :, b * chan : (b + 1) * chan] = copy

    def encode(first):
        window = jnp.concatenate([wide_ref[first + a] for a in range(4)], axis=-1)
        both = jnp.dot(window, pair_w_ref[...], preferred_element_type=jnp.float32)
        both = jnp.maximum(both + enc_b, 0.0)
        keep = [jnp.logical_not((first + d == top) | (first + d == bottom)) for d in range(2)]
        rows = jnp.stack(
            [jnp.where(keep[d], both[:, d * chan : (d + 1) * chan], 0.0) for d in range(2)]
        )
        for b, copy in enumerate(side_copies(rows)):
            enc_ref[pl.ds(first, 2), :, b * chan : (b + 1) * chan] = copy

    @pl.when(step == 0)
    def _():
        for p in range(4):
            for b in range(3):
                k = pl.ds((p * 3 + b) * chan, chan)
                zero = jnp.zeros((chan, chan), jnp.bfloat16)
                pair_w_ref[k, 0:chan] = enc_w_ref[p, b] if p < 3 else zero
                pair_w_ref[k, chan : 2 * chan] = enc_w_ref[p - 1, b] if p > 0 else zero
        put_features(0, low_ref[...])
        put_features(2, own_ref[pl.ds(0, 2)])
        encode(0)

    base = step * ROWS_STEP
    put_features(base + 4, own_ref[pl.ds(base + 2, 2)])

    @pl.when(step < last)
    def _():
        put_features(base + 6, own_ref[pl.ds(base + 4, 2)])

    @pl.when(step == last)
    def _():
        put_features(base + 6, high_ref[...])

    encode(base + 2)
    encode(base + 4)
    cols = own_ref.shape[1]
    row_blocks = cols // BLOCK
    for r in range(0, ROWS_STEP, 2):
        parts = [enc_ref[pl.ds(base + r + a, 2)] for a in range(3)]
        window = jnp.concatenate([v.reshape(2 * cols, 3 * chan) for v in parts], axis=-1)
        hidden = jnp.dot(window, head_w_ref[...], preferred_element_type=jnp.float32)
        hidden = jnp.maximum(hidden + head_b_ref[...], 0.0).astype(jnp.bfloat16)
        raw = jnp.dot(hidden, final_w_ref[...], preferred_element_type=jnp.float32)
        raw = raw + final_b_ref[...]
        norm = jnp.sum(raw * raw, axis=-1, keepdims=True)
        unit = (raw * lax.rsqrt(norm + 1e-06)).astype(jnp.bfloat16)
        all_ref[pl.ds((base + r) * row_blocks, 2 * row_blocks)] = unit.reshape(
            2 * row_blocks, BLOCK, unit.shape[1]
        )
    done = pl.ds(base * row_blocks, ROWS_STEP * row_blocks)
    pltpu.make_async_copy(all_ref.at[done], out_ref.at[done], out_sem).start()

    @pl.when(step == last)
    def _():
        def send(n):
            return pltpu.make_async_copy(all_ref.at[chosen_ref[n]], send_ref.at[n], send_sem)

        def anchor(n):
            return pltpu.make_async_copy(all_ref.at[source_ref[n]], anchor_ref.at[n], anchor_sem)

        @pl.loop(0, send_ref.shape[0])
        def _(n):
            pl.when(chosen_ref[n] >= 0)(lambda: send(n).start())

        pl.loop(0, anchor_ref.shape[0])(lambda n: anchor(n).start())

        @pl.loop(0, send_ref.shape[0])
        def _(n):
            pl.when(chosen_ref[n] >= 0)(lambda: send(n).wait())

        pltpu.make_async_copy(anchor_ref, anchor_ref, anchor_sem).wait()
        pltpu.make_async_copy(all_ref, out_ref, out_sem).wait()


def describe(
    chosen, source, low, own, high, enc_w, enc_b, head_w, head_b, final_w, final_b
):
    rows, cols, chan = own.shape
    desc = final_w.shape[1]
    count = rows * cols // BLOCK
    whole = pl.BlockSpec(memory_space=pltpu.VMEM)
    scalars = pl.BlockSpec(memory_space=pltpu.SMEM)
    macs = rows * cols * (12 * chan * chan + 9 * chan * desc + desc * desc)

    def blocks(n):
        return jax.ShapeDtypeStruct((n, BLOCK, desc), jnp.bfloat16)

    return pl.pallas_call(
        describe_kernel,
        grid=(rows // ROWS_STEP,),
        in_specs=[scalars] * 2 + [whole] * 9,
        out_specs=[pl.BlockSpec(memory_space=pl.ANY)] * 3,
        out_shape=[blocks(count), blocks(chosen.shape[0]), blocks(source.shape[0])],
        scratch_shapes=[
            pltpu.VMEM((rows + 4, cols, 3 * chan), jnp.bfloat16),
            pltpu.VMEM((rows + 2, cols, 3 * chan), jnp.bfloat16),
            pltpu.VMEM((12 * chan, 2 * chan), jnp.bfloat16),
            pltpu.VMEM((count, BLOCK, desc), jnp.bfloat16),
            pltpu.SemaphoreType.DMA,
            pltpu.SemaphoreType.DMA,
            pltpu.SemaphoreType.DMA,
        ],
        compiler_params=pltpu.CompilerParams(vmem_limit_bytes=56 * 2**20),
        cost_estimate=pl.CostEstimate(
            flops=2 * macs, bytes_accessed=rows * cols * (chan + desc) * 2, transcendentals=rows * cols
        ),
    )(
        chosen, source, low, own, high, enc_w, enc_b[None], head_w.reshape(-1, desc),
        head_b[None], final_w, final_b[None],
    )


def match_kernel(slot_ref, anchor_fold_ref, partner_fold_ref, anchor_ref, *refs):
    partners, out_ref = refs[:PAIRS_STEP], refs[-1]
    anchor_fold, partner_fold = anchor_fold_ref[...], partner_fold_ref[...]
    anchor_column, partner_column = jnp.transpose(anchor_fold), jnp.transpose(partner_fold)

    def scores(left, right, left_fold, right_fold):
        products = lax.dot_general(
            left, right, (((1,), (1,)), ((), ())), preferred_element_type=jnp.float32
        )
        return SCORE_SCALE * products - FOLD_PENALTY * (left_fold + right_fold)

    over_i = []
    for n in range(PAIRS_STEP):
        by_i = scores(
            anchor_ref[n], partners[n][0], anchor_column[:, n : n + 1], partner_fold[n : n + 1]
        )
        peak = jnp.max(by_i, axis=0, keepdims=True)
        over_i.append(peak + jnp.log(jnp.sum(jnp.exp(by_i - peak), axis=0, keepdims=True)))
    over_i = jnp.transpose(jnp.concatenate(over_i))
    for n in range(PAIRS_STEP):
        by_j = scores(
            partners[n][0], anchor_ref[n], partner_column[:, n : n + 1], anchor_fold[n : n + 1]
        )
        peak = jnp.max(by_j, axis=0, keepdims=True)
        total = jnp.sum(jnp.exp(by_j - peak), axis=0, keepdims=True)
        best = jnp.max(2.0 * by_j - over_i[:, n : n + 1], axis=0, keepdims=True)
        out_ref[n : n + 1, :] = jnp.exp(best - peak) / total


def match(slot, anchor_folds, partner_folds, anchors, arrived):
    pairs = slot.shape[0]
    shape = (1,) + arrived.shape[1:]
    folds = pl.BlockSpec((PAIRS_STEP, BLOCK), lambda i, s: (i, 0))

    def partner(n):
        return pl.BlockSpec(shape, lambda i, s: (s[i * PAIRS_STEP + n], 0, 0))

    return pl.pallas_call(
        match_kernel,
        grid_spec=pltpu.PrefetchScalarGridSpec(
            num_scalar_prefetch=1,
            grid=(pairs // PAIRS_STEP,),
            in_specs=[folds, folds]
            + [pl.BlockSpec((PAIRS_STEP,) + arrived.shape[1:], lambda i, s: (i, 0, 0))]
            + [partner(n) for n in range(PAIRS_STEP)],
            out_specs=folds,
        ),
        out_shape=jax.ShapeDtypeStruct((pairs, BLOCK), jnp.float32),
        compiler_params=pltpu.CompilerParams(vmem_limit_bytes=32 * 2**20),
    )(slot, anchor_folds, partner_folds, anchors, *([arrived] * PAIRS_STEP))


def local(
    features, fold_mask, encoder_weight, encoder_bias, head_weight, head_bias,
    final_weight, final_bias, pair_source, pair_target,
):
    own_band = features[0]
    band_rows, band_cols, _ = own_band.shape
    desc = final_weight.shape[1]
    tile_count = lax.axis_size("tile")
    tile_here = lax.axis_index("tile")
    section = lax.axis_index("sec")
    swap = [(0, 1), (1, 0)]
    down = [(i, i + 1) for i in range(tile_count - 1)]
    up = [(j, i) for i, j in down]
    low = lax.ppermute(own_band[-2:], "tile", down)
    high = lax.ppermute(own_band[:2], "tile", up)

    block_count = band_rows * band_cols // BLOCK
    pair_count = pair_source.shape[1]
    capacity = max(2, 2 * pair_count // tile_count)
    wanted = lax.dynamic_index_in_dim(pair_target, 1 - section, 0, keepdims=False).reshape(
        tile_count, pair_count
    )
    matched = (wanted // block_count == tile_here).astype(jnp.int32)
    order_rank = jnp.cumsum(matched, axis=1) - matched
    slot_hot = matched[:, :, None] * (
        order_rank[:, :, None] == jnp.arange(capacity)[None, None, :]
    ).astype(jnp.int32)
    chosen = jnp.sum(slot_hot * (wanted % block_count + 1)[:, :, None], axis=1) - 1
    targets = lax.dynamic_index_in_dim(wanted, tile_here, 0, keepdims=False)
    owners = targets // block_count
    earlier = jnp.arange(pair_count)[None, :] < jnp.arange(pair_count)[:, None]
    slot_rank = jnp.sum(((owners[None, :] == owners[:, None]) & earlier).astype(jnp.int32), axis=1)
    slot_index = owners * capacity + slot_rank

    own_folds = fold_mask[0].reshape(block_count, BLOCK).astype(jnp.bfloat16)
    all_folds = lax.all_gather(own_folds, "tile", tiled=True)
    anchor_folds = lax.ppermute(own_folds[pair_source[0]], "sec", swap)

    described, send_blocks, anchors = describe(
        chosen.reshape(-1), pair_source[0], low, own_band, high, encoder_weight, encoder_bias,
        head_weight, head_bias, final_weight, final_bias,
    )
    sibling_anchors = lax.ppermute(anchors, "sec", swap)
    arrived = lax.all_to_all(
        send_blocks.reshape(tile_count, capacity, BLOCK, desc),
        "tile", split_axis=0, concat_axis=0, tiled=True,
    ).reshape(tile_count * capacity, BLOCK, desc)
    confidence = match(
        slot_index,
        anchor_folds.astype(jnp.float32),
        all_folds[targets].astype(jnp.float32),
        sibling_anchors,
        arrived,
    )
    confidence = lax.ppermute(confidence, "sec", swap)
    return (described.reshape(1, band_rows, band_cols, desc), confidence[None])


def solution(mesh):
    return jax.shard_map(
        local,
        mesh=mesh,
        in_specs=(
            P("sec", "tile", None, None), P("sec", "tile", None), P(), P(), P(), P(), P(), P(),
            P("sec", "tile"), P(),
        ),
        out_specs=(P("sec", "tile", None, None), P("sec", "tile", None)),
        check_vma=False,
    )
```

```python
import functools

import jax
import jax.numpy as jnp
from jax import lax
from jax.experimental import pallas as pl
from jax.experimental.pallas import tpu as pltpu
from jax.sharding import PartitionSpec as P

BLOCK = 128
SCORE_SCALE = 10.0
FOLD_PENALTY = 200.0
ROWS_STEP = 8
ENC_PAIRS = 1
DOT_ROWS = 8
PAIRS_STEP = 8


def side_copies(rows):
    cols = rows.shape[1]
    flat = rows.reshape(rows.shape[0] * cols, rows.shape[2])
    column = lax.broadcasted_iota(jnp.int32, rows.shape, 1).reshape(flat.shape)
    before = jnp.where(column == 0, 0.0, pltpu.roll(flat, 1, 0))
    after = jnp.where(column == cols - 1, 0.0, pltpu.roll(flat, flat.shape[0] - 1, 0))
    return [v.reshape(rows.shape).astype(jnp.bfloat16) for v in (before, flat, after)]


def describe_kernel(
    chosen_ref, source_ref, low_ref, own_ref, high_ref, enc_w_ref, enc_b_ref, head_w_ref,
    head_b_ref, final_w_ref, final_b_ref, out_ref, send_ref, anchor_ref, wide_ref, enc_ref,
    pair_w_ref, all_ref, out_sem, send_sem, anchor_sem,
):
    step = pl.program_id(0)
    last = pl.num_programs(0) - 1
    chan = own_ref.shape[2]
    tile_here = lax.axis_index("tile")
    top = jnp.where(tile_here == 0, 0, -1)
    bottom = jnp.where(tile_here == lax.axis_size("tile") - 1, enc_ref.shape[0] - 1, -1)
    enc_b = jnp.concatenate([enc_b_ref[...]] * 2, axis=-1)

    def put_features(first, rows):
        for b, copy in enumerate(side_copies(rows.astype(jnp.float32))):
            wide_ref[pl.ds(first, rows.shape[0]), :, b * chan : (b + 1) * chan] = copy

    def encode(first, pairs):
        window = jnp.concatenate(
            [
                jnp.concatenate([wide_ref[first + 2 * k + a] for a in range(4)], axis=-1)
                for k in range(pairs)
            ]
        )
        both = jnp.dot(window, pair_w_ref[...], preferred_element_type=jnp.float32)
        both = jnp.maximum(both + enc_b, 0.0)
        cols = own_ref.shape[1]
        rows = []
        for d in range(2 * pairs):
            row = both[d // 2 * cols : (d // 2 + 1) * cols, d % 2 * chan : (d % 2 + 1) * chan]
            keep = jnp.logical_not((first + d == top) | (first + d == bottom))
            rows.append(jnp.where(keep, row, 0.0))
        for b, copy in enumerate(side_copies(jnp.stack(rows))):
            enc_ref[pl.ds(first, 2 * pairs), :, b * chan : (b + 1) * chan] = copy

    @pl.when(step == 0)
    def _():
        for p in range(4):
            for b in range(3):
                k = pl.ds((p * 3 + b) * chan, chan)
                zero = jnp.zeros((chan, chan), jnp.bfloat16)
                pair_w_ref[k, 0:chan] = enc_w_ref[p, b] if p < 3 else zero
                pair_w_ref[k, chan : 2 * chan] = enc_w_ref[p - 1, b] if p > 0 else zero
        put_features(0, low_ref[...])
        put_features(2, own_ref[pl.ds(0, 2)])
        encode(0, 1)

    base = step * ROWS_STEP
    put_features(base + 4, own_ref[pl.ds(base + 2, ROWS_STEP - 2)])

    @pl.when(step < last)
    def _():
        put_features(base + ROWS_STEP + 2, own_ref[pl.ds(base + ROWS_STEP, 2)])

    @pl.when(step == last)
    def _():
        put_features(base + ROWS_STEP + 2, high_ref[...])

    for d in range(0, ROWS_STEP, 2 * ENC_PAIRS):
        encode(base + 2 + d, ENC_PAIRS)
    cols = own_ref.shape[1]
    row_blocks = cols // BLOCK
    for r in range(0, ROWS_STEP, DOT_ROWS):
        parts = [enc_ref[pl.ds(base + r + a, DOT_ROWS)] for a in range(3)]
        window = jnp.concatenate([v.reshape(DOT_ROWS * cols, 3 * chan) for v in parts], axis=-1)
        hidden = jnp.dot(window, head_w_ref[...], preferred_element_type=jnp.float32)
        hidden = jnp.maximum(hidden + head_b_ref[...], 0.0).astype(jnp.bfloat16)
        raw = jnp.dot(hidden, final_w_ref[...], preferred_element_type=jnp.float32)
        raw = raw + final_b_ref[...]
        norm = jnp.sum(raw * raw, axis=-1, keepdims=True)
        unit = (raw * lax.rsqrt(norm + 1e-06)).astype(jnp.bfloat16)
        all_ref[pl.ds((base + r) * row_blocks, DOT_ROWS * row_blocks)] = unit.reshape(
            DOT_ROWS * row_blocks, BLOCK, unit.shape[1]
        )
    done = pl.ds(base * row_blocks, ROWS_STEP * row_blocks)
    pltpu.make_async_copy(all_ref.at[done], out_ref.at[done], out_sem).start()

    @pl.when(step == last)
    def _():
        def send(n):
            return pltpu.make_async_copy(all_ref.at[chosen_ref[n]], send_ref.at[n], send_sem)

        def anchor(n):
            return pltpu.make_async_copy(all_ref.at[source_ref[n]], anchor_ref.at[n], anchor_sem)

        @pl.loop(0, send_ref.shape[0])
        def _(n):
            pl.when(chosen_ref[n] >= 0)(lambda: send(n).start())

        pl.loop(0, anchor_ref.shape[0])(lambda n: anchor(n).start())

        @pl.loop(0, send_ref.shape[0])
        def _(n):
            pl.when(chosen_ref[n] >= 0)(lambda: send(n).wait())

        pltpu.make_async_copy(anchor_ref, anchor_ref, anchor_sem).wait()
        pltpu.make_async_copy(all_ref, out_ref, out_sem).wait()


def describe(
    chosen, source, low, own, high, enc_w, enc_b, head_w, head_b, final_w, final_b
):
    rows, cols, chan = own.shape
    desc = final_w.shape[1]
    count = rows * cols // BLOCK
    whole = pl.BlockSpec(memory_space=pltpu.VMEM)
    scalars = pl.BlockSpec(memory_space=pltpu.SMEM)
    macs = rows * cols * (12 * chan * chan + 9 * chan * desc + desc * desc)

    def blocks(n):
        return jax.ShapeDtypeStruct((n, BLOCK, desc), jnp.bfloat16)

    return pl.pallas_call(
        describe_kernel,
        grid=(rows // ROWS_STEP,),
        in_specs=[scalars] * 2 + [whole] * 9,
        out_specs=[pl.BlockSpec(memory_space=pl.ANY)] * 3,
        out_shape=[blocks(count), blocks(chosen.shape[0]), blocks(source.shape[0])],
        scratch_shapes=[
            pltpu.VMEM((rows + 4, cols, 3 * chan), jnp.bfloat16),
            pltpu.VMEM((rows + 2, cols, 3 * chan), jnp.bfloat16),
            pltpu.VMEM((12 * chan, 2 * chan), jnp.bfloat16),
            pltpu.VMEM((count, BLOCK, desc), jnp.bfloat16),
            pltpu.SemaphoreType.DMA,
            pltpu.SemaphoreType.DMA,
            pltpu.SemaphoreType.DMA,
        ],
        compiler_params=pltpu.CompilerParams(vmem_limit_bytes=56 * 2**20),
        cost_estimate=pl.CostEstimate(
            flops=2 * macs, bytes_accessed=rows * cols * (chan + desc) * 2, transcendentals=rows * cols
        ),
    )(
        chosen, source, low, own, high, enc_w, enc_b[None], head_w.reshape(-1, desc),
        head_b[None], final_w, final_b[None],
    )


def match_kernel(slot_ref, anchor_fold_ref, partner_fold_ref, anchor_ref, *refs):
    partners, out_ref = refs[:PAIRS_STEP], refs[-1]
    anchor_fold, partner_fold = anchor_fold_ref[...], partner_fold_ref[...]
    anchor_column, partner_column = jnp.transpose(anchor_fold), jnp.transpose(partner_fold)

    def scores(left, right, left_fold, right_fold):
        products = lax.dot_general(
            left, right, (((1,), (1,)), ((), ())), preferred_element_type=jnp.float32
        )
        return SCORE_SCALE * products - FOLD_PENALTY * (left_fold + right_fold)

    over_i = []
    for n in range(PAIRS_STEP):
        by_i = scores(
            anchor_ref[n], partners[n][0], anchor_column[:, n : n + 1], partner_fold[n : n + 1]
        )
        peak = jnp.max(by_i, axis=0, keepdims=True)
        over_i.append(peak + jnp.log(jnp.sum(jnp.exp(by_i - peak), axis=0, keepdims=True)))
    over_i = jnp.transpose(jnp.concatenate(over_i))
    for n in range(PAIRS_STEP):
        by_j = scores(
            partners[n][0], anchor_ref[n], partner_column[:, n : n + 1], anchor_fold[n : n + 1]
        )
        peak = jnp.max(by_j, axis=0, keepdims=True)
        total = jnp.sum(jnp.exp(by_j - peak), axis=0, keepdims=True)
        best = jnp.max(2.0 * by_j - over_i[:, n : n + 1], axis=0, keepdims=True)
        out_ref[n : n + 1, :] = jnp.exp(best - peak) / total


def match(slot, anchor_folds, partner_folds, anchors, arrived):
    pairs = slot.shape[0]
    shape = (1,) + arrived.shape[1:]
    folds = pl.BlockSpec((PAIRS_STEP, BLOCK), lambda i, s: (i, 0))

    def partner(n):
        return pl.BlockSpec(shape, lambda i, s: (s[i * PAIRS_STEP + n], 0, 0))

    return pl.pallas_call(
        match_kernel,
        grid_spec=pltpu.PrefetchScalarGridSpec(
            num_scalar_prefetch=1,
            grid=(pairs // PAIRS_STEP,),
            in_specs=[folds, folds]
            + [pl.BlockSpec((PAIRS_STEP,) + arrived.shape[1:], lambda i, s: (i, 0, 0))]
            + [partner(n) for n in range(PAIRS_STEP)],
            out_specs=folds,
        ),
        out_shape=jax.ShapeDtypeStruct((pairs, BLOCK), jnp.float32),
        compiler_params=pltpu.CompilerParams(vmem_limit_bytes=32 * 2**20),
    )(slot, anchor_folds, partner_folds, anchors, *([arrived] * PAIRS_STEP))


def local(
    features, fold_mask, encoder_weight, encoder_bias, head_weight, head_bias,
    final_weight, final_bias, pair_source, pair_target,
):
    own_band = features[0]
    band_rows, band_cols, _ = own_band.shape
    desc = final_weight.shape[1]
    tile_count = lax.axis_size("tile")
    tile_here = lax.axis_index("tile")
    section = lax.axis_index("sec")
    swap = [(0, 1), (1, 0)]
    down = [(i, i + 1) for i in range(tile_count - 1)]
    up = [(j, i) for i, j in down]
    low = lax.ppermute(own_band[-2:], "tile", down)
    high = lax.ppermute(own_band[:2], "tile", up)

    block_count = band_rows * band_cols // BLOCK
    pair_count = pair_source.shape[1]
    capacity = max(2, 2 * pair_count // tile_count)
    wanted = lax.dynamic_index_in_dim(pair_target, 1 - section, 0, keepdims=False).reshape(
        tile_count, pair_count
    )
    matched = (wanted // block_count == tile_here).astype(jnp.int32)
    order_rank = jnp.cumsum(matched, axis=1) - matched
    slot_hot = matched[:, :, None] * (
        order_rank[:, :, None] == jnp.arange(capacity)[None, None, :]
    ).astype(jnp.int32)
    chosen = jnp.sum(slot_hot * (wanted % block_count + 1)[:, :, None], axis=1) - 1
    targets = lax.dynamic_index_in_dim(wanted, tile_here, 0, keepdims=False)
    owners = targets // block_count
    earlier = jnp.arange(pair_count)[None, :] < jnp.arange(pair_count)[:, None]
    slot_rank = jnp.sum(((owners[None, :] == owners[:, None]) & earlier).astype(jnp.int32), axis=1)
    slot_index = owners * capacity + slot_rank

    own_folds = fold_mask[0].reshape(block_count, BLOCK).astype(jnp.bfloat16)
    all_folds = lax.all_gather(own_folds, "tile", tiled=True)
    anchor_folds = lax.ppermute(own_folds[pair_source[0]], "sec", swap)

    described, send_blocks, anchors = describe(
        chosen.reshape(-1), pair_source[0], low, own_band, high, encoder_weight, encoder_bias,
        head_weight, head_bias, final_weight, final_bias,
    )
    send_blocks, all_folds = lax.optimization_barrier((send_blocks, all_folds))
    sibling_anchors = lax.ppermute(anchors, "sec", swap)
    arrived = lax.all_to_all(
        send_blocks.reshape(tile_count, capacity, BLOCK, desc),
        "tile", split_axis=0, concat_axis=0, tiled=True,
    ).reshape(tile_count * capacity, BLOCK, desc)
    confidence = match(
        slot_index,
        anchor_folds.astype(jnp.float32),
        all_folds[targets].astype(jnp.float32),
        sibling_anchors,
        arrived,
    )
    confidence = lax.ppermute(confidence, "sec", swap)
    return (described.reshape(1, band_rows, band_cols, desc), confidence[None])


def solution(mesh):
    return jax.shard_map(
        local,
        mesh=mesh,
        in_specs=(
            P("sec", "tile", None, None), P("sec", "tile", None), P(), P(), P(), P(), P(), P(),
            P("sec", "tile"), P(),
        ),
        out_specs=(P("sec", "tile", None, None), P("sec", "tile", None)),
        check_vma=False,
    )
```

```python
import functools

import jax
import jax.numpy as jnp
from jax import lax
from jax.experimental import pallas as pl
from jax.experimental.pallas import tpu as pltpu
from jax.sharding import PartitionSpec as P

BLOCK = 128
SCORE_SCALE = 10.0
FOLD_PENALTY = 200.0
ROWS_STEP = 8
ENC_PAIRS = 1
DOT_ROWS = 8
PAIRS_STEP = 16
VMEM_MATCH = 56 * 2**20


def side_copies(rows):
    cols = rows.shape[1]
    flat = rows.reshape(rows.shape[0] * cols, rows.shape[2])
    column = lax.broadcasted_iota(jnp.int32, rows.shape, 1).reshape(flat.shape)
    before = jnp.where(column == 0, 0.0, pltpu.roll(flat, 1, 0))
    after = jnp.where(column == cols - 1, 0.0, pltpu.roll(flat, flat.shape[0] - 1, 0))
    return [v.reshape(rows.shape).astype(jnp.bfloat16) for v in (before, flat, after)]


def describe_kernel(
    chosen_ref, source_ref, low_ref, own_ref, high_ref, enc_w_ref, enc_b_ref, head_w_ref,
    head_b_ref, final_w_ref, final_b_ref, out_ref, send_ref, anchor_ref, wide_ref, enc_ref,
    pair_w_ref, all_ref, out_sem, send_sem, anchor_sem,
):
    step = pl.program_id(0)
    last = pl.num_programs(0) - 1
    chan = own_ref.shape[2]
    tile_here = lax.axis_index("tile")
    top = jnp.where(tile_here == 0, 0, -1)
    bottom = jnp.where(tile_here == lax.axis_size("tile") - 1, enc_ref.shape[0] - 1, -1)
    enc_b = jnp.concatenate([enc_b_ref[...]] * 2, axis=-1)

    def put_features(first, rows):
        for b, copy in enumerate(side_copies(rows.astype(jnp.float32))):
            wide_ref[pl.ds(first, rows.shape[0]), :, b * chan : (b + 1) * chan] = copy

    def encode(first, pairs):
        window = jnp.concatenate(
            [
                jnp.concatenate([wide_ref[first + 2 * k + a] for a in range(4)], axis=-1)
                for k in range(pairs)
            ]
        )
        both = jnp.dot(window, pair_w_ref[...], preferred_element_type=jnp.float32)
        both = jnp.maximum(both + enc_b, 0.0)
        cols = own_ref.shape[1]
        rows = []
        for d in range(2 * pairs):
            row = both[d // 2 * cols : (d // 2 + 1) * cols, d % 2 * chan : (d % 2 + 1) * chan]
            keep = jnp.logical_not((first + d == top) | (first + d == bottom))
            rows.append(jnp.where(keep, row, 0.0))
        for b, copy in enumerate(side_copies(jnp.stack(rows))):
            enc_ref[pl.ds(first, 2 * pairs), :, b * chan : (b + 1) * chan] = copy

    @pl.when(step == 0)
    def _():
        for p in range(4):
            for b in range(3):
                k = pl.ds((p * 3 + b) * chan, chan)
                zero = jnp.zeros((chan, chan), jnp.bfloat16)
                pair_w_ref[k, 0:chan] = enc_w_ref[p, b] if p < 3 else zero
                pair_w_ref[k, chan : 2 * chan] = enc_w_ref[p - 1, b] if p > 0 else zero
        put_features(0, low_ref[...])
        put_features(2, own_ref[pl.ds(0, 2)])
        encode(0, 1)

    base = step * ROWS_STEP
    put_features(base + 4, own_ref[pl.ds(base + 2, ROWS_STEP - 2)])

    @pl.when(step < last)
    def _():
        put_features(base + ROWS_STEP + 2, own_ref[pl.ds(base + ROWS_STEP, 2)])

    @pl.when(step == last)
    def _():
        put_features(base + ROWS_STEP + 2, high_ref[...])

    for d in range(0, ROWS_STEP, 2 * ENC_PAIRS):
        encode(base + 2 + d, ENC_PAIRS)
    cols = own_ref.shape[1]
    row_blocks = cols // BLOCK
    for r in range(0, ROWS_STEP, DOT_ROWS):
        parts = [enc_ref[pl.ds(base + r + a, DOT_ROWS)] for a in range(3)]
        window = jnp.concatenate([v.reshape(DOT_ROWS * cols, 3 * chan) for v in parts], axis=-1)
        hidden = jnp.dot(window, head_w_ref[...], preferred_element_type=jnp.float32)
        hidden = jnp.maximum(hidden + head_b_ref[...], 0.0).astype(jnp.bfloat16)
        raw = jnp.dot(hidden, final_w_ref[...], preferred_element_type=jnp.float32)
        raw = raw + final_b_ref[...]
        norm = jnp.sum(raw * raw, axis=-1, keepdims=True)
        unit = (raw * lax.rsqrt(norm + 1e-06)).astype(jnp.bfloat16)
        all_ref[pl.ds((base + r) * row_blocks, DOT_ROWS * row_blocks)] = unit.reshape(
            DOT_ROWS * row_blocks, BLOCK, unit.shape[1]
        )
    done = pl.ds(base * row_blocks, ROWS_STEP * row_blocks)
    pltpu.make_async_copy(all_ref.at[done], out_ref.at[done], out_sem).start()

    @pl.when(step == last)
    def _():
        def send(n):
            return pltpu.make_async_copy(all_ref.at[chosen_ref[n]], send_ref.at[n], send_sem)

        def anchor(n):
            return pltpu.make_async_copy(all_ref.at[source_ref[n]], anchor_ref.at[n], anchor_sem)

        @pl.loop(0, send_ref.shape[0])
        def _(n):
            pl.when(chosen_ref[n] >= 0)(lambda: send(n).start())

        pl.loop(0, anchor_ref.shape[0])(lambda n: anchor(n).start())

        @pl.loop(0, send_ref.shape[0])
        def _(n):
            pl.when(chosen_ref[n] >= 0)(lambda: send(n).wait())

        pltpu.make_async_copy(anchor_ref, anchor_ref, anchor_sem).wait()
        pltpu.make_async_copy(all_ref, out_ref, out_sem).wait()


def describe(
    chosen, source, low, own, high, enc_w, enc_b, head_w, head_b, final_w, final_b
):
    rows, cols, chan = own.shape
    desc = final_w.shape[1]
    count = rows * cols // BLOCK
    whole = pl.BlockSpec(memory_space=pltpu.VMEM)
    scalars = pl.BlockSpec(memory_space=pltpu.SMEM)
    macs = rows * cols * (12 * chan * chan + 9 * chan * desc + desc * desc)

    def blocks(n):
        return jax.ShapeDtypeStruct((n, BLOCK, desc), jnp.bfloat16)

    return pl.pallas_call(
        describe_kernel,
        grid=(rows // ROWS_STEP,),
        in_specs=[scalars] * 2 + [whole] * 9,
        out_specs=[pl.BlockSpec(memory_space=pl.ANY)] * 3,
        out_shape=[blocks(count), blocks(chosen.shape[0]), blocks(source.shape[0])],
        scratch_shapes=[
            pltpu.VMEM((rows + 4, cols, 3 * chan), jnp.bfloat16),
            pltpu.VMEM((rows + 2, cols, 3 * chan), jnp.bfloat16),
            pltpu.VMEM((12 * chan, 2 * chan), jnp.bfloat16),
            pltpu.VMEM((count, BLOCK, desc), jnp.bfloat16),
            pltpu.SemaphoreType.DMA,
            pltpu.SemaphoreType.DMA,
            pltpu.SemaphoreType.DMA,
        ],
        compiler_params=pltpu.CompilerParams(vmem_limit_bytes=56 * 2**20),
        cost_estimate=pl.CostEstimate(
            flops=2 * macs, bytes_accessed=rows * cols * (chan + desc) * 2, transcendentals=rows * cols
        ),
    )(
        chosen, source, low, own, high, enc_w, enc_b[None], head_w.reshape(-1, desc),
        head_b[None], final_w, final_b[None],
    )


def match_kernel(
    slot_ref, anchor_fold_ref, partner_fold_ref, anchors_ref, arrived_ref, out_ref, anchor_ref,
    partner_ref, anchor_sem, partner_sem,
):
    groups = out_ref.shape[0] // PAIRS_STEP

    def products(left, right):
        return SCORE_SCALE * lax.dot_general(
            left, right, (((1,), (1,)), ((), ())), preferred_element_type=jnp.float32
        )

    def group(g):
        return pl.ds(g * PAIRS_STEP, PAIRS_STEP)

    def anchors(g):
        return pltpu.make_async_copy(
            anchors_ref.at[group(g)], anchor_ref.at[group(g)], anchor_sem.at[g]
        )

    @pl.loop(0, groups)
    def _(g):
        anchors(g).start()
        for n in range(PAIRS_STEP):
            pair = g * PAIRS_STEP + n
            pltpu.make_async_copy(
                arrived_ref.at[slot_ref[pair]], partner_ref.at[pair], partner_sem.at[g]
            ).start()

    @pl.loop(0, groups)
    def _(g):
        anchor_cost = FOLD_PENALTY * anchor_fold_ref[group(g)]
        anchor_column = jnp.transpose(anchor_cost)
        partner_column = jnp.transpose(FOLD_PENALTY * partner_fold_ref[group(g)])
        anchors(g).wait()
        here = partner_ref.at[group(g)]
        pltpu.make_async_copy(here, here, partner_sem.at[g]).wait()
        left = [anchor_ref[g * PAIRS_STEP + n] for n in range(PAIRS_STEP)]
        right = [partner_ref[g * PAIRS_STEP + n] for n in range(PAIRS_STEP)]

        over_i = []
        for n in range(PAIRS_STEP):
            by_i = products(left[n], right[n]) - anchor_column[:, n : n + 1]
            peak = jnp.max(by_i, axis=0, keepdims=True)
            over_i.append(peak + jnp.log(jnp.sum(jnp.exp(by_i - peak), axis=0, keepdims=True)))
        over_i = jnp.transpose(jnp.concatenate(over_i))
        result = []
        for n in range(PAIRS_STEP):
            plain = products(right[n], left[n])
            by_j = plain - partner_column[:, n : n + 1]
            peak = jnp.max(by_j, axis=0, keepdims=True)
            total = jnp.sum(jnp.exp(by_j - peak), axis=0, keepdims=True)
            best = jnp.max(by_j + (plain - over_i[:, n : n + 1]), axis=0, keepdims=True)
            result.append(jnp.exp(best - peak - anchor_cost[n : n + 1]) / total)
        out_ref[group(g)] = jnp.concatenate(result)


def match(slot, anchor_folds, partner_folds, anchors, arrived):
    pairs = slot.shape[0]
    whole = pl.BlockSpec(memory_space=pltpu.VMEM)
    return pl.pallas_call(
        match_kernel,
        in_specs=[pl.BlockSpec(memory_space=pltpu.SMEM), whole, whole]
        + [pl.BlockSpec(memory_space=pl.ANY)] * 2,
        out_specs=whole,
        out_shape=jax.ShapeDtypeStruct((pairs, BLOCK), jnp.float32),
        scratch_shapes=[pltpu.VMEM(anchors.shape, jnp.bfloat16)] * 2
        + [pltpu.SemaphoreType.DMA((pairs // PAIRS_STEP,))] * 2,
        compiler_params=pltpu.CompilerParams(vmem_limit_bytes=VMEM_MATCH),
    )(slot, anchor_folds, partner_folds, anchors, arrived)


def local(
    features, fold_mask, encoder_weight, encoder_bias, head_weight, head_bias,
    final_weight, final_bias, pair_source, pair_target,
):
    own_band = features[0]
    band_rows, band_cols, _ = own_band.shape
    desc = final_weight.shape[1]
    tile_count = lax.axis_size("tile")
    tile_here = lax.axis_index("tile")
    section = lax.axis_index("sec")
    swap = [(0, 1), (1, 0)]
    down = [(i, i + 1) for i in range(tile_count - 1)]
    up = [(j, i) for i, j in down]
    low = lax.ppermute(own_band[-2:], "tile", down)
    high = lax.ppermute(own_band[:2], "tile", up)

    block_count = band_rows * band_cols // BLOCK
    pair_count = pair_source.shape[1]
    capacity = max(2, 2 * pair_count // tile_count)
    wanted = lax.dynamic_index_in_dim(pair_target, 1 - section, 0, keepdims=False).reshape(
        tile_count, pair_count
    )
    matched = (wanted // block_count == tile_here).astype(jnp.int32)
    order_rank = jnp.cumsum(matched, axis=1) - matched
    slot_hot = matched[:, :, None] * (
        order_rank[:, :, None] == jnp.arange(capacity)[None, None, :]
    ).astype(jnp.int32)
    chosen = jnp.sum(slot_hot * (wanted % block_count + 1)[:, :, None], axis=1) - 1
    targets = lax.dynamic_index_in_dim(wanted, tile_here, 0, keepdims=False)
    owners = targets // block_count
    earlier = jnp.arange(pair_count)[None, :] < jnp.arange(pair_count)[:, None]
    slot_rank = jnp.sum(((owners[None, :] == owners[:, None]) & earlier).astype(jnp.int32), axis=1)
    slot_index = owners * capacity + slot_rank

    own_folds = fold_mask[0].reshape(block_count, BLOCK).astype(jnp.bfloat16)
    send_folds = own_folds[jnp.maximum(chosen, 0)]
    anchor_folds = own_folds[pair_source[0]]

    described, send_blocks, anchors = describe(
        chosen.reshape(-1), pair_source[0], low, own_band, high, encoder_weight, encoder_bias,
        head_weight, head_bias, final_weight, final_bias,
    )
    arrived = lax.all_to_all(
        send_blocks.reshape(tile_count, capacity, BLOCK, desc),
        "tile", split_axis=0, concat_axis=0, tiled=True,
    ).reshape(tile_count * capacity, BLOCK, desc)
    sibling_anchors = lax.ppermute(anchors, "sec", swap)
    send_folds, anchor_folds, sibling_anchors = lax.optimization_barrier(
        (send_folds, anchor_folds, sibling_anchors)
    )
    anchor_folds = lax.ppermute(anchor_folds, "sec", swap)
    partner_folds = lax.all_to_all(
        send_folds, "tile", split_axis=0, concat_axis=0, tiled=True
    ).reshape(tile_count * capacity, BLOCK)[slot_index]
    confidence = match(
        slot_index,
        anchor_folds.astype(jnp.float32),
        partner_folds.astype(jnp.float32),
        sibling_anchors,
        arrived,
    )
    confidence = lax.ppermute(confidence, "sec", swap)
    return (described.reshape(1, band_rows, band_cols, desc), confidence[None])


def solution(mesh):
    return jax.shard_map(
        local,
        mesh=mesh,
        in_specs=(
            P("sec", "tile", None, None), P("sec", "tile", None), P(), P(), P(), P(), P(), P(),
            P("sec", "tile"), P(),
        ),
        out_specs=(P("sec", "tile", None, None), P("sec", "tile", None)),
        check_vma=False,
    )
```

```python
import functools

import jax
import jax.numpy as jnp
from jax import lax
from jax.experimental import pallas as pl
from jax.experimental.pallas import tpu as pltpu
from jax.sharding import PartitionSpec as P

BLOCK = 128
SCORE_SCALE = 10.0
FOLD_PENALTY = 200.0
ROWS_STEP = 8
ENC_PAIRS = 1
DOT_ROWS = 8
PAIRS_STEP = 16
VMEM_MATCH = 56 * 2**20


def side_copies(rows):
    cols = rows.shape[1]
    flat = rows.reshape(rows.shape[0] * cols, rows.shape[2])
    column = lax.broadcasted_iota(jnp.int32, rows.shape, 1).reshape(flat.shape)
    before = jnp.where(column == 0, 0.0, pltpu.roll(flat, 1, 0))
    after = jnp.where(column == cols - 1, 0.0, pltpu.roll(flat, flat.shape[0] - 1, 0))
    return [v.reshape(rows.shape).astype(jnp.bfloat16) for v in (before, flat, after)]


def describe_kernel(
    chosen_ref, source_ref, low_ref, own_ref, high_ref, enc_w_ref, enc_b_ref, head_w_ref,
    head_b_ref, final_w_ref, final_b_ref, out_ref, send_ref, anchor_ref, wide_ref, enc_ref,
    pair_w_ref, all_ref, out_sem, send_sem, anchor_sem,
):
    step = pl.program_id(0)
    last = pl.num_programs(0) - 1
    chan = own_ref.shape[2]
    tile_here = lax.axis_index("tile")
    top = jnp.where(tile_here == 0, 0, -1)
    bottom = jnp.where(tile_here == lax.axis_size("tile") - 1, enc_ref.shape[0] - 1, -1)
    enc_b = jnp.concatenate([enc_b_ref[...]] * 2, axis=-1)

    def put_features(first, rows):
        for b, copy in enumerate(side_copies(rows.astype(jnp.float32))):
            wide_ref[pl.ds(first, rows.shape[0]), :, b * chan : (b + 1) * chan] = copy

    def encode(first, pairs):
        window = jnp.concatenate(
            [
                jnp.concatenate([wide_ref[first + 2 * k + a] for a in range(4)], axis=-1)
                for k in range(pairs)
            ]
        )
        both = jnp.dot(window, pair_w_ref[...], preferred_element_type=jnp.float32)
        both = jnp.maximum(both + enc_b, 0.0)
        cols = own_ref.shape[1]
        rows = []
        for d in range(2 * pairs):
            row = both[d // 2 * cols : (d // 2 + 1) * cols, d % 2 * chan : (d % 2 + 1) * chan]
            keep = jnp.logical_not((first + d == top) | (first + d == bottom))
            rows.append(jnp.where(keep, row, 0.0))
        for b, copy in enumerate(side_copies(jnp.stack(rows))):
            enc_ref[pl.ds(first, 2 * pairs), :, b * chan : (b + 1) * chan] = copy

    @pl.when(step == 0)
    def _():
        for p in range(4):
            for b in range(3):
                k = pl.ds((p * 3 + b) * chan, chan)
                zero = jnp.zeros((chan, chan), jnp.bfloat16)
                pair_w_ref[k, 0:chan] = enc_w_ref[p, b] if p < 3 else zero
                pair_w_ref[k, chan : 2 * chan] = enc_w_ref[p - 1, b] if p > 0 else zero
        put_features(0, low_ref[...])
        put_features(2, own_ref[pl.ds(0, 2)])
        encode(0, 1)

    base = step * ROWS_STEP
    put_features(base + 4, own_ref[pl.ds(base + 2, ROWS_STEP - 2)])

    @pl.when(step < last)
    def _():
        put_features(base + ROWS_STEP + 2, own_ref[pl.ds(base + ROWS_STEP, 2)])

    @pl.when(step == last)
    def _():
        put_features(base + ROWS_STEP + 2, high_ref[...])

    for d in range(0, ROWS_STEP, 2 * ENC_PAIRS):
        encode(base + 2 + d, ENC_PAIRS)
    cols = own_ref.shape[1]
    row_blocks = cols // BLOCK
    for r in range(0, ROWS_STEP, DOT_ROWS):
        parts = [enc_ref[pl.ds(base + r + a, DOT_ROWS)] for a in range(3)]
        window = jnp.concatenate([v.reshape(DOT_ROWS * cols, 3 * chan) for v in parts], axis=-1)
        hidden = jnp.dot(window, head_w_ref[...], preferred_element_type=jnp.float32)
        hidden = jnp.maximum(hidden + head_b_ref[...], 0.0).astype(jnp.bfloat16)
        raw = jnp.dot(hidden, final_w_ref[...], preferred_element_type=jnp.float32)
        raw = raw + final_b_ref[...]
        norm = jnp.sum(raw * raw, axis=-1, keepdims=True)
        unit = (raw * lax.rsqrt(norm + 1e-06)).astype(jnp.bfloat16)
        all_ref[pl.ds((base + r) * row_blocks, DOT_ROWS * row_blocks)] = unit.reshape(
            DOT_ROWS * row_blocks, BLOCK, unit.shape[1]
        )
    done = pl.ds(base * row_blocks, ROWS_STEP * row_blocks)
    pltpu.make_async_copy(all_ref.at[done], out_ref.at[done], out_sem).start()

    @pl.when(step == last)
    def _():
        def send(n):
            return pltpu.make_async_copy(all_ref.at[chosen_ref[n]], send_ref.at[n], send_sem)

        def anchor(n):
            return pltpu.make_async_copy(all_ref.at[source_ref[n]], anchor_ref.at[n], anchor_sem)

        @pl.loop(0, send_ref.shape[0])
        def _(n):
            pl.when(chosen_ref[n] >= 0)(lambda: send(n).start())

        pl.loop(0, anchor_ref.shape[0])(lambda n: anchor(n).start())

        @pl.loop(0, send_ref.shape[0])
        def _(n):
            pl.when(chosen_ref[n] >= 0)(lambda: send(n).wait())

        pltpu.make_async_copy(anchor_ref, anchor_ref, anchor_sem).wait()
        pltpu.make_async_copy(all_ref, out_ref, out_sem).wait()


def describe(
    chosen, source, low, own, high, enc_w, enc_b, head_w, head_b, final_w, final_b
):
    rows, cols, chan = own.shape
    desc = final_w.shape[1]
    count = rows * cols // BLOCK
    whole = pl.BlockSpec(memory_space=pltpu.VMEM)
    scalars = pl.BlockSpec(memory_space=pltpu.SMEM)
    macs = rows * cols * (12 * chan * chan + 9 * chan * desc + desc * desc)

    def blocks(n):
        return jax.ShapeDtypeStruct((n, BLOCK, desc), jnp.bfloat16)

    return pl.pallas_call(
        describe_kernel,
        grid=(rows // ROWS_STEP,),
        in_specs=[scalars] * 2 + [whole] * 9,
        out_specs=[pl.BlockSpec(memory_space=pl.ANY)] * 3,
        out_shape=[blocks(count), blocks(chosen.shape[0]), blocks(source.shape[0])],
        scratch_shapes=[
            pltpu.VMEM((rows + 4, cols, 3 * chan), jnp.bfloat16),
            pltpu.VMEM((rows + 2, cols, 3 * chan), jnp.bfloat16),
            pltpu.VMEM((12 * chan, 2 * chan), jnp.bfloat16),
            pltpu.VMEM((count, BLOCK, desc), jnp.bfloat16),
            pltpu.SemaphoreType.DMA,
            pltpu.SemaphoreType.DMA,
            pltpu.SemaphoreType.DMA,
        ],
        compiler_params=pltpu.CompilerParams(vmem_limit_bytes=56 * 2**20),
        cost_estimate=pl.CostEstimate(
            flops=2 * macs, bytes_accessed=rows * cols * (chan + desc) * 2, transcendentals=rows * cols
        ),
    )(
        chosen, source, low, own, high, enc_w, enc_b[None], head_w.reshape(-1, desc),
        head_b[None], final_w, final_b[None],
    )


def match_kernel(
    slot_ref, anchor_fold_ref, partner_fold_ref, anchors_ref, arrived_ref, out_ref, anchor_ref,
    partner_ref, anchor_sem, partner_sem,
):
    groups = out_ref.shape[0] // PAIRS_STEP

    def products(left, right):
        return SCORE_SCALE * lax.dot_general(
            left, right, (((1,), (1,)), ((), ())), preferred_element_type=jnp.float32
        )

    def group(g):
        return pl.ds(g * PAIRS_STEP, PAIRS_STEP)

    def anchors(g):
        return pltpu.make_async_copy(
            anchors_ref.at[group(g)], anchor_ref.at[group(g)], anchor_sem.at[g]
        )

    @pl.loop(0, groups)
    def _(g):
        anchors(g).start()
        for n in range(PAIRS_STEP):
            pair = g * PAIRS_STEP + n
            pltpu.make_async_copy(
                arrived_ref.at[slot_ref[pair]], partner_ref.at[pair], partner_sem.at[g]
            ).start()

    @pl.loop(0, groups)
    def _(g):
        anchor_cost = FOLD_PENALTY * anchor_fold_ref[group(g)]
        anchor_column = jnp.transpose(anchor_cost)
        partner_column = jnp.transpose(FOLD_PENALTY * partner_fold_ref[group(g)])
        anchors(g).wait()
        here = partner_ref.at[group(g)]
        pltpu.make_async_copy(here, here, partner_sem.at[g]).wait()
        left = [anchor_ref[g * PAIRS_STEP + n] for n in range(PAIRS_STEP)]
        right = [partner_ref[g * PAIRS_STEP + n] for n in range(PAIRS_STEP)]

        over_i = []
        for n in range(PAIRS_STEP):
            by_i = products(left[n], right[n]) - anchor_column[:, n : n + 1]
            peak = jnp.max(by_i, axis=0, keepdims=True)
            over_i.append(peak + jnp.log(jnp.sum(jnp.exp(by_i - peak), axis=0, keepdims=True)))
        over_i = jnp.transpose(jnp.concatenate(over_i))
        result = []
        for n in range(PAIRS_STEP):
            plain = products(right[n], left[n])
            by_j = plain - partner_column[:, n : n + 1]
            peak = jnp.max(by_j, axis=0, keepdims=True)
            total = jnp.sum(jnp.exp(by_j - peak), axis=0, keepdims=True)
            best = jnp.max(by_j + (plain - over_i[:, n : n + 1]), axis=0, keepdims=True)
            result.append(jnp.exp(best - peak - anchor_cost[n : n + 1]) / total)
        out_ref[group(g)] = jnp.concatenate(result)


def match(slot, anchor_folds, partner_folds, anchors, arrived):
    pairs = slot.shape[0]
    whole = pl.BlockSpec(memory_space=pltpu.VMEM)
    return pl.pallas_call(
        match_kernel,
        in_specs=[pl.BlockSpec(memory_space=pltpu.SMEM), whole, whole]
        + [pl.BlockSpec(memory_space=pl.ANY)] * 2,
        out_specs=whole,
        out_shape=jax.ShapeDtypeStruct((pairs, BLOCK), jnp.float32),
        scratch_shapes=[pltpu.VMEM(anchors.shape, jnp.bfloat16)] * 2
        + [pltpu.SemaphoreType.DMA((pairs // PAIRS_STEP,))] * 2,
        compiler_params=pltpu.CompilerParams(vmem_limit_bytes=VMEM_MATCH),
    )(slot, anchor_folds, partner_folds, anchors, arrived)


def local(
    features, fold_mask, encoder_weight, encoder_bias, head_weight, head_bias,
    final_weight, final_bias, pair_source, pair_target,
):
    own_band = features[0]
    band_rows, band_cols, _ = own_band.shape
    desc = final_weight.shape[1]
    tile_count = lax.axis_size("tile")
    tile_here = lax.axis_index("tile")
    section = lax.axis_index("sec")
    swap = [(0, 1), (1, 0)]
    down = [(i, i + 1) for i in range(tile_count - 1)]
    up = [(j, i) for i, j in down]
    low = lax.ppermute(own_band[-2:], "tile", down)
    high = lax.ppermute(own_band[:2], "tile", up)

    block_count = band_rows * band_cols // BLOCK
    pair_count = pair_source.shape[1]
    capacity = max(2, 2 * pair_count // tile_count)
    wanted = lax.dynamic_index_in_dim(pair_target, 1 - section, 0, keepdims=False).reshape(
        tile_count, pair_count
    )
    matched = (wanted // block_count == tile_here).astype(jnp.int32)
    order_rank = jnp.cumsum(matched, axis=1) - matched
    slot_hot = matched[:, :, None] * (
        order_rank[:, :, None] == jnp.arange(capacity)[None, None, :]
    ).astype(jnp.int32)
    chosen = jnp.sum(slot_hot * (wanted % block_count + 1)[:, :, None], axis=1) - 1
    targets = lax.dynamic_index_in_dim(wanted, tile_here, 0, keepdims=False)
    owners = targets // block_count
    earlier = jnp.arange(pair_count)[None, :] < jnp.arange(pair_count)[:, None]
    slot_rank = jnp.sum(((owners[None, :] == owners[:, None]) & earlier).astype(jnp.int32), axis=1)
    slot_index = owners * capacity + slot_rank

    own_folds = fold_mask[0].reshape(block_count, BLOCK).astype(jnp.bfloat16)
    partner_folds = lax.all_to_all(
        own_folds[jnp.maximum(chosen, 0)], "tile", split_axis=0, concat_axis=0, tiled=True
    )
    anchor_folds = lax.ppermute(own_folds[pair_source[0]], "sec", swap)

    described, send_blocks, anchors = describe(
        chosen.reshape(-1), pair_source[0], low, own_band, high, encoder_weight, encoder_bias,
        head_weight, head_bias, final_weight, final_bias,
    )
    anchors, partner_folds, anchor_folds = lax.optimization_barrier(
        (anchors, partner_folds, anchor_folds)
    )
    sibling_anchors = lax.ppermute(anchors, "sec", swap)
    partner_folds = partner_folds.reshape(tile_count * capacity, BLOCK)[slot_index]
    partner_folds = partner_folds.astype(jnp.float32)
    anchor_folds = anchor_folds.astype(jnp.float32)
    send_blocks, sibling_anchors, slot_index, partner_folds, anchor_folds = lax.optimization_barrier(
        (send_blocks, sibling_anchors, slot_index, partner_folds, anchor_folds)
    )
    arrived = lax.all_to_all(
        send_blocks.reshape(tile_count, capacity, BLOCK, desc),
        "tile", split_axis=0, concat_axis=0, tiled=True,
    ).reshape(tile_count * capacity, BLOCK, desc)
    confidence = match(slot_index, anchor_folds, partner_folds, sibling_anchors, arrived)
    confidence = lax.ppermute(confidence, "sec", swap)
    return (described.reshape(1, band_rows, band_cols, desc), confidence[None])


def solution(mesh):
    return jax.shard_map(
        local,
        mesh=mesh,
        in_specs=(
            P("sec", "tile", None, None), P("sec", "tile", None), P(), P(), P(), P(), P(), P(),
            P("sec", "tile"), P(),
        ),
        out_specs=(P("sec", "tile", None, None), P("sec", "tile", None)),
        check_vma=False,
    )
```

```python
import functools

import jax
import jax.numpy as jnp
from jax import lax
from jax.experimental import pallas as pl
from jax.experimental.pallas import tpu as pltpu
from jax.sharding import PartitionSpec as P

BLOCK = 128
SCORE_SCALE = 10.0
FOLD_PENALTY = 200.0
ROWS_STEP = 8
FOLD_ROWS = 16
ENC_PAIRS = 1
DOT_ROWS = 8
PAIRS_STEP = 16
VMEM_MATCH = 56 * 2**20


def side_copies(rows):
    cols = rows.shape[1]
    flat = rows.reshape(rows.shape[0] * cols, rows.shape[2])
    column = lax.broadcasted_iota(jnp.int32, rows.shape, 1).reshape(flat.shape)
    before = jnp.where(column == 0, 0.0, pltpu.roll(flat, 1, 0))
    after = jnp.where(column == cols - 1, 0.0, pltpu.roll(flat, flat.shape[0] - 1, 0))
    return [v.reshape(rows.shape).astype(jnp.bfloat16) for v in (before, flat, after)]


def describe_kernel(
    chosen_ref, source_ref, chosen_row_ref, source_row_ref, fold_ref, low_ref, own_ref, high_ref, enc_w_ref, enc_b_ref, head_w_ref,
    head_b_ref, final_w_ref, final_b_ref, out_ref, send_ref, anchor_ref, wide_ref, enc_ref,
    pair_w_ref, all_ref, send_fold_ref, anchor_fold_ref, out_sem, send_sem, anchor_sem,
    fold_sem,
):
    step = pl.program_id(0)
    last = pl.num_programs(0) - 1
    chan = own_ref.shape[2]
    tile_here = lax.axis_index("tile")
    top = jnp.where(tile_here == 0, 0, -1)
    bottom = jnp.where(tile_here == lax.axis_size("tile") - 1, enc_ref.shape[0] - 1, -1)
    enc_b = jnp.concatenate([enc_b_ref[...]] * 2, axis=-1)

    def put_features(first, rows):
        for b, copy in enumerate(side_copies(rows.astype(jnp.float32))):
            wide_ref[pl.ds(first, rows.shape[0]), :, b * chan : (b + 1) * chan] = copy

    def encode(first, pairs):
        window = jnp.concatenate(
            [
                jnp.concatenate([wide_ref[first + 2 * k + a] for a in range(4)], axis=-1)
                for k in range(pairs)
            ]
        )
        both = jnp.dot(window, pair_w_ref[...], preferred_element_type=jnp.float32)
        both = jnp.maximum(both + enc_b, 0.0)
        cols = own_ref.shape[1]
        rows = []
        for d in range(2 * pairs):
            row = both[d // 2 * cols : (d // 2 + 1) * cols, d % 2 * chan : (d % 2 + 1) * chan]
            keep = jnp.logical_not((first + d == top) | (first + d == bottom))
            rows.append(jnp.where(keep, row, 0.0))
        for b, copy in enumerate(side_copies(jnp.stack(rows))):
            enc_ref[pl.ds(first, 2 * pairs), :, b * chan : (b + 1) * chan] = copy

    cols = own_ref.shape[1]
    row_blocks = cols // BLOCK
    pairs = source_ref.shape[0]
    peers = send_ref.shape[0]

    def send(n):
        place = send_ref.at[n % peers, pl.ds(pl.multiple_of(n // peers * BLOCK, BLOCK), BLOCK)]
        return pltpu.make_async_copy(all_ref.at[chosen_ref[n]], place, send_sem)

    def anchor(n):
        return pltpu.make_async_copy(all_ref.at[source_ref[n]], anchor_ref.at[n], anchor_sem)

    def ship(first, end):
        @pl.loop(0, chosen_ref.shape[0], unroll=4)
        def _(n):
            pl.when((chosen_ref[n] >= first) & (chosen_ref[n] < end))(lambda: send(n).start())

        @pl.loop(0, pairs, unroll=4)
        def _(n):
            pl.when((source_ref[n] >= first) & (source_ref[n] < end))(lambda: anchor(n).start())

    def fold_copies():
        return (
            pltpu.make_async_copy(
                send_fold_ref, send_ref.at[:, pl.ds(2 * BLOCK, FOLD_ROWS)], fold_sem.at[0]
            ),
            pltpu.make_async_copy(
                anchor_fold_ref, anchor_ref.at[pairs, pl.ds(0, pairs), pl.ds(0, BLOCK)], fold_sem.at[1]
            ),
        )

    @pl.when(step == 1)
    def _():
        stacked = jnp.concatenate(
            [fold_ref[:, c * BLOCK : (c + 1) * BLOCK] for c in range(row_blocks)]
        ).astype(jnp.float32)
        order = lax.broadcasted_iota(jnp.int32, (stacked.shape[0], 1), 0)
        block = lax.rem(order, fold_ref.shape[0]) * row_blocks + order // fold_ref.shape[0]

        def picked(row):
            return lax.dot_general(
                (block == row).astype(jnp.float32), stacked, (((0,), (0,)), ((), ())),
                preferred_element_type=jnp.float32,
            )

        rows = picked(chosen_row_ref[...])
        both = jnp.concatenate([rows[:peers], rows[peers:]], axis=-1)
        send_fold_ref[...] = jnp.broadcast_to(both[:, None], send_fold_ref.shape).astype(jnp.bfloat16)
        anchor_fold_ref[...] = picked(source_row_ref[...]).astype(jnp.bfloat16)
        for copy in fold_copies():
            copy.start()

    @pl.when(step == 0)
    def _():
        for p in range(4):
            for b in range(3):
                k = pl.ds((p * 3 + b) * chan, chan)
                zero = jnp.zeros((chan, chan), jnp.bfloat16)
                pair_w_ref[k, 0:chan] = enc_w_ref[p, b] if p < 3 else zero
                pair_w_ref[k, chan : 2 * chan] = enc_w_ref[p - 1, b] if p > 0 else zero
        put_features(0, low_ref[...])
        put_features(2, own_ref[pl.ds(0, 2)])
        encode(0, 1)

    base = step * ROWS_STEP
    put_features(base + 4, own_ref[pl.ds(base + 2, ROWS_STEP - 2)])

    @pl.when(step < last)
    def _():
        put_features(base + ROWS_STEP + 2, own_ref[pl.ds(base + ROWS_STEP, 2)])

    @pl.when(step == last)
    def _():
        put_features(base + ROWS_STEP + 2, high_ref[...])

    for d in range(0, ROWS_STEP, 2 * ENC_PAIRS):
        encode(base + 2 + d, ENC_PAIRS)
    for r in range(0, ROWS_STEP, DOT_ROWS):
        parts = [enc_ref[pl.ds(base + r + a, DOT_ROWS)] for a in range(3)]
        window = jnp.concatenate([v.reshape(DOT_ROWS * cols, 3 * chan) for v in parts], axis=-1)
        hidden = jnp.dot(window, head_w_ref[...], preferred_element_type=jnp.float32)
        hidden = jnp.maximum(hidden + head_b_ref[...], 0.0).astype(jnp.bfloat16)
        raw = jnp.dot(hidden, final_w_ref[...], preferred_element_type=jnp.float32)
        raw = raw + final_b_ref[...]
        norm = jnp.sum(raw * raw, axis=-1, keepdims=True)
        unit = (raw * lax.rsqrt(norm + 1e-06)).astype(jnp.bfloat16)
        all_ref[pl.ds((base + r) * row_blocks, DOT_ROWS * row_blocks)] = unit.reshape(
            DOT_ROWS * row_blocks, BLOCK, unit.shape[1]
        )
    done = pl.ds(base * row_blocks, ROWS_STEP * row_blocks)
    pltpu.make_async_copy(all_ref.at[done], out_ref.at[done], out_sem).start()

    @pl.when(step == last)
    def _():
        ship(0, all_ref.shape[0])

        @pl.loop(0, chosen_ref.shape[0], unroll=4)
        def _(n):
            pl.when(chosen_ref[n] >= 0)(lambda: send(n).wait())

        every = anchor_ref.at[pl.ds(0, source_ref.shape[0])]
        pltpu.make_async_copy(every, every, anchor_sem).wait()
        for copy in fold_copies():
            copy.wait()
        pltpu.make_async_copy(all_ref, out_ref, out_sem).wait()


def describe(
    chosen, source, folds, low, own, high, enc_w, enc_b, head_w, head_b, final_w, final_b
):
    rows, cols, chan = own.shape
    desc = final_w.shape[1]
    count = rows * cols // BLOCK
    whole = pl.BlockSpec(memory_space=pltpu.VMEM)
    scalars = pl.BlockSpec(memory_space=pltpu.SMEM)
    macs = rows * cols * (12 * chan * chan + 9 * chan * desc + desc * desc)

    def blocks(n, height):
        return jax.ShapeDtypeStruct((n, height, desc), jnp.bfloat16)

    return pl.pallas_call(
        describe_kernel,
        grid=(rows // ROWS_STEP,),
        in_specs=[scalars] * 2 + [whole] * 12,
        out_specs=[pl.BlockSpec(memory_space=pl.ANY)] * 3,
        out_shape=[
            blocks(count, BLOCK),
            blocks(chosen.shape[0] // 2, 2 * BLOCK + FOLD_ROWS),
            blocks(source.shape[0] + 1, BLOCK),
        ],
        scratch_shapes=[
            pltpu.VMEM((rows + 4, cols, 3 * chan), jnp.bfloat16),
            pltpu.VMEM((rows + 2, cols, 3 * chan), jnp.bfloat16),
            pltpu.VMEM((12 * chan, 2 * chan), jnp.bfloat16),
            pltpu.VMEM((count, BLOCK, desc), jnp.bfloat16),
            pltpu.VMEM((chosen.shape[0] // 2, FOLD_ROWS, desc), jnp.bfloat16),
            pltpu.VMEM((source.shape[0], BLOCK), jnp.bfloat16),
            pltpu.SemaphoreType.DMA,
            pltpu.SemaphoreType.DMA,
            pltpu.SemaphoreType.DMA,
            pltpu.SemaphoreType.DMA((2,)),
        ],
        compiler_params=pltpu.CompilerParams(vmem_limit_bytes=56 * 2**20),
        cost_estimate=pl.CostEstimate(
            flops=2 * macs, bytes_accessed=rows * cols * (chan + desc) * 2, transcendentals=rows * cols
        ),
    )(
        chosen, source, chosen[None], source[None], folds, low, own, high, enc_w, enc_b[None], head_w.reshape(-1, desc),
        head_b[None], final_w, final_b[None],
    )


def match_kernel(
    slot_ref, anchors_ref, arrived_ref, out_ref, anchor_ref, partner_ref, anchor_fold_ref,
    partner_fold_ref, anchor_sem, partner_sem, fold_sem,
):
    groups = out_ref.shape[0] // PAIRS_STEP

    def products(left, right):
        return SCORE_SCALE * lax.dot_general(
            left, right, (((1,), (1,)), ((), ())), preferred_element_type=jnp.float32
        )

    def group(g):
        return pl.ds(g * PAIRS_STEP, PAIRS_STEP)

    def anchors(g):
        return pltpu.make_async_copy(
            anchors_ref.at[group(g)], anchor_ref.at[group(g)], anchor_sem.at[g]
        )

    pairs = out_ref.shape[0]
    fold_copies = (
        pltpu.make_async_copy(
            arrived_ref.at[:, pl.ds(2 * BLOCK, FOLD_ROWS)], partner_fold_ref, fold_sem.at[0]
        ),
        pltpu.make_async_copy(
            anchors_ref.at[pairs, pl.ds(0, pairs), pl.ds(0, BLOCK)], anchor_fold_ref, fold_sem.at[1]
        ),
    )
    for copy in fold_copies:
        copy.start()

    def place(pair):
        return slot_ref[pair] // 2, pl.multiple_of(slot_ref[pair] % 2 * BLOCK, BLOCK)

    @pl.loop(0, groups)
    def _(g):
        anchors(g).start()
        for n in range(PAIRS_STEP):
            pair = g * PAIRS_STEP + n
            owner, start = place(pair)
            pltpu.make_async_copy(
                arrived_ref.at[owner, pl.ds(start, BLOCK)], partner_ref.at[pair], partner_sem.at[g]
            ).start()

    for copy in fold_copies:
        copy.wait()

    @pl.loop(0, groups)
    def _(g):
        anchor_cost = FOLD_PENALTY * anchor_fold_ref[group(g)].astype(jnp.float32)
        anchor_column = jnp.transpose(anchor_cost)
        partner_cost = []
        for n in range(PAIRS_STEP):
            owner, start = place(g * PAIRS_STEP + n)
            both = partner_fold_ref[owner].astype(jnp.float32)
            tile = jnp.where(start == 0, both[:, :BLOCK], both[:, BLOCK:])
            partner_cost.append(tile[:1])
        partner_column = jnp.transpose(FOLD_PENALTY * jnp.concatenate(partner_cost))
        anchors(g).wait()
        here = partner_ref.at[group(g)]
        pltpu.make_async_copy(here, here, partner_sem.at[g]).wait()
        left = [anchor_ref[g * PAIRS_STEP + n] for n in range(PAIRS_STEP)]
        right = [partner_ref[g * PAIRS_STEP + n] for n in range(PAIRS_STEP)]

        over_i = []
        for n in range(PAIRS_STEP):
            by_i = products(left[n], right[n]) - anchor_column[:, n : n + 1]
            peak = jnp.max(by_i, axis=0, keepdims=True)
            over_i.append(peak + jnp.log(jnp.sum(jnp.exp(by_i - peak), axis=0, keepdims=True)))
        over_i = jnp.transpose(jnp.concatenate(over_i))
        result = []
        for n in range(PAIRS_STEP):
            plain = products(right[n], left[n])
            by_j = plain - partner_column[:, n : n + 1]
            peak = jnp.max(by_j, axis=0, keepdims=True)
            total = jnp.sum(jnp.exp(by_j - peak), axis=0, keepdims=True)
            best = jnp.max(by_j + (plain - over_i[:, n : n + 1]), axis=0, keepdims=True)
            result.append(jnp.exp(best - peak - anchor_cost[n : n + 1]) / total)
        out_ref[group(g)] = jnp.concatenate(result)


def match(slot, anchors, arrived):
    pairs = slot.shape[0]
    desc = arrived.shape[2]
    return pl.pallas_call(
        match_kernel,
        in_specs=[pl.BlockSpec(memory_space=pltpu.SMEM)] + [pl.BlockSpec(memory_space=pl.ANY)] * 2,
        out_specs=pl.BlockSpec(memory_space=pltpu.VMEM),
        out_shape=jax.ShapeDtypeStruct((pairs, BLOCK), jnp.float32),
        scratch_shapes=[pltpu.VMEM((pairs, BLOCK, desc), jnp.bfloat16)] * 2
        + [
            pltpu.VMEM((pairs, BLOCK), jnp.bfloat16),
            pltpu.VMEM((arrived.shape[0], FOLD_ROWS, desc), jnp.bfloat16),
        ]
        + [pltpu.SemaphoreType.DMA((pairs // PAIRS_STEP,))] * 2
        + [pltpu.SemaphoreType.DMA((2,))],
        compiler_params=pltpu.CompilerParams(vmem_limit_bytes=VMEM_MATCH),
    )(slot, anchors, arrived)


def local(
    features, fold_mask, encoder_weight, encoder_bias, head_weight, head_bias,
    final_weight, final_bias, pair_source, pair_target,
):
    own_band = features[0]
    band_rows, band_cols, _ = own_band.shape
    tile_count = lax.axis_size("tile")
    tile_here = lax.axis_index("tile")
    section = lax.axis_index("sec")
    swap = [(0, 1), (1, 0)]
    down = [(i, i + 1) for i in range(tile_count - 1)]
    up = [(j, i) for i, j in down]
    low = lax.ppermute(own_band[-2:], "tile", down)
    high = lax.ppermute(own_band[:2], "tile", up)

    block_count = band_rows * band_cols // BLOCK
    pair_count = pair_source.shape[1]
    capacity = 2
    wanted = lax.dynamic_index_in_dim(pair_target, 1 - section, 0, keepdims=False).reshape(
        tile_count, pair_count
    )
    matched = (wanted // block_count == tile_here).astype(jnp.int32)
    order_rank = jnp.cumsum(matched, axis=1) - matched
    slot_hot = matched[None] * (
        order_rank[None] == jnp.arange(capacity)[:, None, None]
    ).astype(jnp.int32)
    chosen = jnp.sum(slot_hot * (wanted % block_count + 1)[None], axis=2) - 1
    targets = lax.dynamic_index_in_dim(wanted, tile_here, 0, keepdims=False)
    owners = targets // block_count
    earlier = jnp.arange(pair_count)[None, :] < jnp.arange(pair_count)[:, None]
    slot_rank = jnp.sum(((owners[None, :] == owners[:, None]) & earlier).astype(jnp.int32), axis=1)
    slot_index = owners * capacity + slot_rank

    described, send_blocks, anchors = describe(
        chosen.reshape(-1), pair_source[0], fold_mask[0], low, own_band, high, encoder_weight,
        encoder_bias, head_weight, head_bias, final_weight, final_bias,
    )
    sibling_anchors = lax.ppermute(anchors, "sec", swap)
    send_blocks, sibling_anchors, slot_index = lax.optimization_barrier(
        (send_blocks, sibling_anchors, slot_index)
    )
    arrived = lax.all_to_all(send_blocks, "tile", split_axis=0, concat_axis=0, tiled=True)
    confidence = match(slot_index, sibling_anchors, arrived)
    confidence = lax.ppermute(confidence, "sec", swap)
    return (described.reshape(1, band_rows, band_cols, -1), confidence[None])


def solution(mesh):
    return jax.shard_map(
        local,
        mesh=mesh,
        in_specs=(
            P("sec", "tile", None, None), P("sec", "tile", None), P(), P(), P(), P(), P(), P(),
            P("sec", "tile"), P(),
        ),
        out_specs=(P("sec", "tile", None, None), P("sec", "tile", None)),
        check_vma=False,
    )
```

```python
import functools

import jax
import jax.numpy as jnp
from jax import lax
from jax.experimental import pallas as pl
from jax.experimental.pallas import tpu as pltpu
from jax.sharding import PartitionSpec as P

BLOCK = 128
SCORE_SCALE = 10.0
FOLD_PENALTY = 200.0
ROWS_STEP = 8
FOLD_ROWS = 16
LANES = 128
ENC_PAIRS = 1
DOT_ROWS = 8
PAIRS_STEP = 16
VMEM_MATCH = 56 * 2**20


def side_copies(rows):
    cols = rows.shape[1]
    flat = rows.reshape(rows.shape[0] * cols, rows.shape[2])
    column = lax.broadcasted_iota(jnp.int32, rows.shape, 1).reshape(flat.shape)
    before = jnp.where(column == 0, 0.0, pltpu.roll(flat, 1, 0))
    after = jnp.where(column == cols - 1, 0.0, pltpu.roll(flat, flat.shape[0] - 1, 0))
    return [v.reshape(rows.shape).astype(jnp.bfloat16) for v in (before, flat, after)]


def describe_kernel(
    chosen_ref, source_ref, chosen_row_ref, source_row_ref, fold_ref, low_ref, own_ref, high_ref, enc_w_ref, enc_b_ref, head_w_ref,
    head_b_ref, final_w_ref, final_b_ref, out_ref, send_ref, anchor_ref, wide_ref, enc_ref,
    pair_w_ref, all_ref, send_fold_ref, anchor_fold_ref, out_sem, send_sem, anchor_sem,
    fold_sem,
):
    step = pl.program_id(0)
    last = pl.num_programs(0) - 1
    chan = own_ref.shape[2]
    tile_here = lax.axis_index("tile")
    top = jnp.where(tile_here == 0, 0, -1)
    bottom = jnp.where(tile_here == lax.axis_size("tile") - 1, enc_ref.shape[0] - 1, -1)
    enc_b = jnp.concatenate([enc_b_ref[...]] * 2, axis=-1)

    def put_features(first, rows):
        for b, copy in enumerate(side_copies(rows.astype(jnp.float32))):
            wide_ref[pl.ds(first, rows.shape[0]), :, b * chan : (b + 1) * chan] = copy

    def encode(first, pairs):
        window = jnp.concatenate(
            [
                jnp.concatenate([wide_ref[first + 2 * k + a] for a in range(4)], axis=-1)
                for k in range(pairs)
            ]
        )
        both = jnp.dot(window, pair_w_ref[...], preferred_element_type=jnp.float32)
        both = jnp.maximum(both + enc_b, 0.0)
        cols = own_ref.shape[1]
        rows = []
        for d in range(2 * pairs):
            row = both[d // 2 * cols : (d // 2 + 1) * cols, d % 2 * chan : (d % 2 + 1) * chan]
            keep = jnp.logical_not((first + d == top) | (first + d == bottom))
            rows.append(jnp.where(keep, row, 0.0))
        for b, copy in enumerate(side_copies(jnp.stack(rows))):
            enc_ref[pl.ds(first, 2 * pairs), :, b * chan : (b + 1) * chan] = copy

    cols = own_ref.shape[1]
    row_blocks = cols // BLOCK
    pairs = source_ref.shape[0]
    peers = send_ref.shape[0]

    def send(n):
        start = pl.multiple_of(n // peers * 2 * BLOCK, 2 * BLOCK)
        place = send_ref.at[n % peers, pl.ds(start, 2 * BLOCK)]
        return pltpu.make_async_copy(all_ref.at[chosen_ref[n]], place, send_sem)

    def anchor(n):
        return pltpu.make_async_copy(all_ref.at[source_ref[n]], anchor_ref.at[n], anchor_sem)

    def ship(first, end):
        @pl.loop(0, chosen_ref.shape[0], unroll=4)
        def _(n):
            pl.when((chosen_ref[n] >= first) & (chosen_ref[n] < end))(lambda: send(n).start())

        @pl.loop(0, pairs, unroll=4)
        def _(n):
            pl.when((source_ref[n] >= first) & (source_ref[n] < end))(lambda: anchor(n).start())

    def fold_copies():
        return (
            pltpu.make_async_copy(
                send_fold_ref, send_ref.at[:, pl.ds(4 * BLOCK, FOLD_ROWS)], fold_sem.at[0]
            ),
            pltpu.make_async_copy(
                anchor_fold_ref, anchor_ref.at[pairs, pl.ds(0, pairs)], fold_sem.at[1]
            ),
        )

    @pl.when(step == 1)
    def _():
        stacked = jnp.concatenate(
            [fold_ref[:, c * BLOCK : (c + 1) * BLOCK] for c in range(row_blocks)]
        ).astype(jnp.float32)
        order = lax.broadcasted_iota(jnp.int32, (stacked.shape[0], 1), 0)
        block = lax.rem(order, fold_ref.shape[0]) * row_blocks + order // fold_ref.shape[0]

        def picked(row):
            return lax.dot_general(
                (block == row).astype(jnp.float32), stacked, (((0,), (0,)), ((), ())),
                preferred_element_type=jnp.float32,
            )

        rows = picked(chosen_row_ref[...])
        place = lax.broadcasted_iota(jnp.int32, send_fold_ref.shape, 1)
        both = jnp.where(place == 0, rows[:peers][:, None], rows[peers:][:, None])
        send_fold_ref[...] = both.astype(jnp.bfloat16)
        anchor_fold_ref[...] = picked(source_row_ref[...]).astype(jnp.bfloat16)
        for copy in fold_copies():
            copy.start()

    @pl.when(step == 0)
    def _():
        for p in range(4):
            for b in range(3):
                k = pl.ds((p * 3 + b) * chan, chan)
                zero = jnp.zeros((chan, chan), jnp.bfloat16)
                pair_w_ref[k, 0:chan] = enc_w_ref[p, b] if p < 3 else zero
                pair_w_ref[k, chan : 2 * chan] = enc_w_ref[p - 1, b] if p > 0 else zero
        put_features(0, low_ref[...])
        put_features(2, own_ref[pl.ds(0, 2)])
        encode(0, 1)

    base = step * ROWS_STEP
    put_features(base + 4, own_ref[pl.ds(base + 2, ROWS_STEP - 2)])

    @pl.when(step < last)
    def _():
        put_features(base + ROWS_STEP + 2, own_ref[pl.ds(base + ROWS_STEP, 2)])

    @pl.when(step == last)
    def _():
        put_features(base + ROWS_STEP + 2, high_ref[...])

    for d in range(0, ROWS_STEP, 2 * ENC_PAIRS):
        encode(base + 2 + d, ENC_PAIRS)
    for r in range(0, ROWS_STEP, DOT_ROWS):
        parts = [enc_ref[pl.ds(base + r + a, DOT_ROWS)] for a in range(3)]
        window = jnp.concatenate([v.reshape(DOT_ROWS * cols, 3 * chan) for v in parts], axis=-1)
        hidden = jnp.dot(window, head_w_ref[...], preferred_element_type=jnp.float32)
        hidden = jnp.maximum(hidden + head_b_ref[...], 0.0).astype(jnp.bfloat16)
        raw = jnp.dot(hidden, final_w_ref[...], preferred_element_type=jnp.float32)
        raw = raw + final_b_ref[...]
        norm = jnp.sum(raw * raw, axis=-1, keepdims=True)
        unit = (raw * lax.rsqrt(norm + 1e-06)).astype(jnp.bfloat16)
        place = pl.ds((base + r) * row_blocks, DOT_ROWS * row_blocks)
        for h in range(2):
            all_ref[place, h * BLOCK : (h + 1) * BLOCK] = unit[:, h * LANES : (h + 1) * LANES].reshape(
                DOT_ROWS * row_blocks, BLOCK, LANES
            )
    done = pl.ds(base * row_blocks, ROWS_STEP * row_blocks)
    for h in range(2):
        pltpu.make_async_copy(
            all_ref.at[done, pl.ds(h * BLOCK, BLOCK)],
            out_ref.at[done, :, pl.ds(h * LANES, LANES)],
            out_sem,
        ).start()

    @pl.when(step == last)
    def _():
        ship(0, all_ref.shape[0])

        @pl.loop(0, chosen_ref.shape[0], unroll=4)
        def _(n):
            pl.when(chosen_ref[n] >= 0)(lambda: send(n).wait())

        every = anchor_ref.at[pl.ds(0, source_ref.shape[0])]
        pltpu.make_async_copy(every, every, anchor_sem).wait()
        for copy in fold_copies():
            copy.wait()
        pltpu.make_async_copy(all_ref, all_ref, out_sem).wait()


def describe(
    chosen, source, folds, low, own, high, enc_w, enc_b, head_w, head_b, final_w, final_b
):
    rows, cols, chan = own.shape
    desc = final_w.shape[1]
    count = rows * cols // BLOCK
    whole = pl.BlockSpec(memory_space=pltpu.VMEM)
    scalars = pl.BlockSpec(memory_space=pltpu.SMEM)
    macs = rows * cols * (12 * chan * chan + 9 * chan * desc + desc * desc)

    def half_lanes(n, height):
        return jax.ShapeDtypeStruct((n, height, LANES), jnp.bfloat16)

    return pl.pallas_call(
        describe_kernel,
        grid=(rows // ROWS_STEP,),
        in_specs=[scalars] * 2 + [whole] * 12,
        out_specs=[pl.BlockSpec(memory_space=pl.ANY)] * 3,
        out_shape=[
            jax.ShapeDtypeStruct((count, BLOCK, desc), jnp.bfloat16),
            half_lanes(chosen.shape[0] // 2, 4 * BLOCK + FOLD_ROWS),
            half_lanes(source.shape[0] + 1, 2 * BLOCK),
        ],
        scratch_shapes=[
            pltpu.VMEM((rows + 4, cols, 3 * chan), jnp.bfloat16),
            pltpu.VMEM((rows + 2, cols, 3 * chan), jnp.bfloat16),
            pltpu.VMEM((12 * chan, 2 * chan), jnp.bfloat16),
            pltpu.VMEM((count, 2 * BLOCK, LANES), jnp.bfloat16),
            pltpu.VMEM((chosen.shape[0] // 2, FOLD_ROWS, LANES), jnp.bfloat16),
            pltpu.VMEM((source.shape[0], BLOCK), jnp.bfloat16),
            pltpu.SemaphoreType.DMA,
            pltpu.SemaphoreType.DMA,
            pltpu.SemaphoreType.DMA,
            pltpu.SemaphoreType.DMA((2,)),
        ],
        compiler_params=pltpu.CompilerParams(vmem_limit_bytes=56 * 2**20),
        cost_estimate=pl.CostEstimate(
            flops=2 * macs, bytes_accessed=rows * cols * (chan + desc) * 2, transcendentals=rows * cols
        ),
    )(
        chosen, source, chosen[None], source[None], folds, low, own, high, enc_w, enc_b[None], head_w.reshape(-1, desc),
        head_b[None], final_w, final_b[None],
    )


def match_kernel(
    slot_ref, anchors_ref, arrived_ref, out_ref, anchor_ref, partner_ref, anchor_fold_ref,
    partner_fold_ref, anchor_sem, partner_sem, fold_sem,
):
    groups = out_ref.shape[0] // PAIRS_STEP

    def products(left, right):
        return SCORE_SCALE * lax.dot_general(
            left, right, (((1,), (1,)), ((), ())), preferred_element_type=jnp.float32
        )

    def group(g):
        return pl.ds(g * PAIRS_STEP, PAIRS_STEP)

    def anchors(g):
        return pltpu.make_async_copy(
            anchors_ref.at[group(g)], anchor_ref.at[group(g)], anchor_sem.at[g]
        )

    pairs = out_ref.shape[0]
    fold_copies = (
        pltpu.make_async_copy(
            arrived_ref.at[:, pl.ds(4 * BLOCK, FOLD_ROWS)], partner_fold_ref, fold_sem.at[0]
        ),
        pltpu.make_async_copy(
            anchors_ref.at[pairs, pl.ds(0, pairs)], anchor_fold_ref, fold_sem.at[1]
        ),
    )
    for copy in fold_copies:
        copy.start()

    def place(pair):
        return slot_ref[pair] // 2, pl.multiple_of(slot_ref[pair] % 2 * 2 * BLOCK, 2 * BLOCK)

    @pl.loop(0, groups)
    def _(g):
        anchors(g).start()
        for n in range(PAIRS_STEP):
            pair = g * PAIRS_STEP + n
            owner, start = place(pair)
            pltpu.make_async_copy(
                arrived_ref.at[owner, pl.ds(start, 2 * BLOCK)], partner_ref.at[pair], partner_sem.at[g]
            ).start()

    for copy in fold_copies:
        copy.wait()

    @pl.loop(0, groups)
    def _(g):
        anchor_cost = FOLD_PENALTY * anchor_fold_ref[group(g)].astype(jnp.float32)
        anchor_column = jnp.transpose(anchor_cost)
        partner_cost = []
        for n in range(PAIRS_STEP):
            owner, start = place(g * PAIRS_STEP + n)
            both = partner_fold_ref[owner].astype(jnp.float32)
            partner_cost.append(jnp.where(start == 0, both[0:1], both[1:2]))
        partner_column = jnp.transpose(FOLD_PENALTY * jnp.concatenate(partner_cost))
        anchors(g).wait()
        here = partner_ref.at[group(g)]
        pltpu.make_async_copy(here, here, partner_sem.at[g]).wait()
        left, right = [
            [
                jnp.concatenate([ref[g * PAIRS_STEP + n, h * BLOCK : (h + 1) * BLOCK] for h in range(2)], axis=1)
                for n in range(PAIRS_STEP)
            ]
            for ref in (anchor_ref, partner_ref)
        ]

        over_i = []
        for n in range(PAIRS_STEP):
            by_i = products(left[n], right[n]) - anchor_column[:, n : n + 1]
            peak = jnp.max(by_i, axis=0, keepdims=True)
            over_i.append(peak + jnp.log(jnp.sum(jnp.exp(by_i - peak), axis=0, keepdims=True)))
        over_i = jnp.transpose(jnp.concatenate(over_i))
        result = []
        for n in range(PAIRS_STEP):
            plain = products(right[n], left[n])
            by_j = plain - partner_column[:, n : n + 1]
            peak = jnp.max(by_j, axis=0, keepdims=True)
            total = jnp.sum(jnp.exp(by_j - peak), axis=0, keepdims=True)
            best = jnp.max(by_j + (plain - over_i[:, n : n + 1]), axis=0, keepdims=True)
            result.append(jnp.exp(best - peak - anchor_cost[n : n + 1]) / total)
        out_ref[group(g)] = jnp.concatenate(result)


def match(slot, anchors, arrived):
    pairs = slot.shape[0]
    return pl.pallas_call(
        match_kernel,
        in_specs=[pl.BlockSpec(memory_space=pltpu.SMEM)] + [pl.BlockSpec(memory_space=pl.ANY)] * 2,
        out_specs=pl.BlockSpec(memory_space=pltpu.VMEM),
        out_shape=jax.ShapeDtypeStruct((pairs, BLOCK), jnp.float32),
        scratch_shapes=[pltpu.VMEM((pairs, 2 * BLOCK, LANES), jnp.bfloat16)] * 2
        + [
            pltpu.VMEM((pairs, BLOCK), jnp.bfloat16),
            pltpu.VMEM((arrived.shape[0], FOLD_ROWS, LANES), jnp.bfloat16),
        ]
        + [pltpu.SemaphoreType.DMA((pairs // PAIRS_STEP,))] * 2
        + [pltpu.SemaphoreType.DMA((2,))],
        compiler_params=pltpu.CompilerParams(vmem_limit_bytes=VMEM_MATCH),
    )(slot, anchors, arrived)


def local(
    features, fold_mask, encoder_weight, encoder_bias, head_weight, head_bias,
    final_weight, final_bias, pair_source, pair_target,
):
    own_band = features[0]
    band_rows, band_cols, _ = own_band.shape
    tile_count = lax.axis_size("tile")
    tile_here = lax.axis_index("tile")
    section = lax.axis_index("sec")
    swap = [(0, 1), (1, 0)]
    down = [(i, i + 1) for i in range(tile_count - 1)]
    up = [(j, i) for i, j in down]
    low = lax.ppermute(own_band[-2:], "tile", down)
    high = lax.ppermute(own_band[:2], "tile", up)

    block_count = band_rows * band_cols // BLOCK
    pair_count = pair_source.shape[1]
    capacity = 2
    wanted = lax.dynamic_index_in_dim(pair_target, 1 - section, 0, keepdims=False).reshape(
        tile_count, pair_count
    )
    matched = (wanted // block_count == tile_here).astype(jnp.int32)
    order_rank = jnp.cumsum(matched, axis=1) - matched
    slot_hot = matched[None] * (
        order_rank[None] == jnp.arange(capacity)[:, None, None]
    ).astype(jnp.int32)
    chosen = jnp.sum(slot_hot * (wanted % block_count + 1)[None], axis=2) - 1
    targets = lax.dynamic_index_in_dim(wanted, tile_here, 0, keepdims=False)
    owners = targets // block_count
    earlier = jnp.arange(pair_count)[None, :] < jnp.arange(pair_count)[:, None]
    slot_rank = jnp.sum(((owners[None, :] == owners[:, None]) & earlier).astype(jnp.int32), axis=1)
    slot_index = owners * capacity + slot_rank

    described, send_blocks, anchors = describe(
        chosen.reshape(-1), pair_source[0], fold_mask[0], low, own_band, high, encoder_weight,
        encoder_bias, head_weight, head_bias, final_weight, final_bias,
    )
    sibling_anchors = lax.ppermute(anchors, "sec", swap)
    send_blocks, sibling_anchors, slot_index = lax.optimization_barrier(
        (send_blocks, sibling_anchors, slot_index)
    )
    arrived = lax.all_to_all(send_blocks, "tile", split_axis=0, concat_axis=0, tiled=True)
    confidence = match(slot_index, sibling_anchors, arrived)
    confidence = lax.ppermute(confidence, "sec", swap)
    return (described.reshape(1, band_rows, band_cols, -1), confidence[None])


def solution(mesh):
    return jax.shard_map(
        local,
        mesh=mesh,
        in_specs=(
            P("sec", "tile", None, None), P("sec", "tile", None), P(), P(), P(), P(), P(), P(),
            P("sec", "tile"), P(),
        ),
        out_specs=(P("sec", "tile", None, None), P("sec", "tile", None)),
        check_vma=False,
    )
```

```python
import functools

import jax
import jax.numpy as jnp
from jax import lax
from jax.experimental import pallas as pl
from jax.experimental.pallas import tpu as pltpu
from jax.sharding import PartitionSpec as P

BLOCK = 128
SCORE_SCALE = 10.0
FOLD_PENALTY = 200.0
LOG2_E = 1.4426950408889634
ROWS_STEP = 8
FOLD_ROWS = 16
LANES = 128
ENC_PAIRS = 1
DOT_ROWS = 8
PAIRS_STEP = 32
VMEM_MATCH = 56 * 2**20


def side_copies(rows):
    cols = rows.shape[1]
    flat = rows.reshape(rows.shape[0] * cols, rows.shape[2])
    column = lax.broadcasted_iota(jnp.int32, rows.shape, 1).reshape(flat.shape)
    before = jnp.where(column == 0, 0.0, pltpu.roll(flat, 1, 0))
    after = jnp.where(column == cols - 1, 0.0, pltpu.roll(flat, flat.shape[0] - 1, 0))
    return [v.reshape(rows.shape).astype(jnp.bfloat16) for v in (before, flat, after)]


def describe_kernel(
    chosen_ref, source_ref, chosen_row_ref, source_row_ref, fold_ref, low_ref, own_ref, high_ref,
    enc_w_hbm, enc_b_ref, head_w_hbm, head_b_ref, final_w_hbm, final_b_ref, out_ref, send_ref,
    anchor_ref, feature_ref, enc_w_ref, head_w_ref, final_w_ref, in_sem, weight_sem, wide_ref,
    enc_ref, pair_w_ref, all_ref, send_fold_ref, anchor_fold_ref, out_sem, send_sem, anchor_sem,
    fold_sem,
):
    step = pl.program_id(0)
    last = pl.num_programs(0) - 1
    chan = own_ref.shape[2]
    height = own_ref.shape[0]
    steps = height // ROWS_STEP
    tile_here = lax.axis_index("tile")
    top = jnp.where(tile_here == 0, 0, -1)
    bottom = jnp.where(tile_here == lax.axis_size("tile") - 1, enc_ref.shape[0] - 1, -1)
    enc_b = jnp.concatenate([enc_b_ref[...]] * 2, axis=-1)

    def feature_copies(i):
        first = 0 if i == 0 else i * ROWS_STEP + 2
        end = min((i + 1) * ROWS_STEP + 2, height)
        parts = [(own_ref.at[pl.ds(first, end - first)], first + 2)]
        if i == 0:
            parts.append((low_ref, 0))
        if i == steps - 1:
            parts.append((high_ref, height + 2))
        return [
            pltpu.make_async_copy(
                part, feature_ref.at[pl.ds(place, part.shape[0])], in_sem.at[2 * i + n]
            )
            for n, (part, place) in enumerate(parts)
        ]

    weight_copies = [
        pltpu.make_async_copy(source, place, weight_sem.at[n])
        for n, (source, place) in enumerate(
            ((enc_w_hbm, enc_w_ref), (head_w_hbm, head_w_ref), (final_w_hbm, final_w_ref))
        )
    ]

    @pl.when(step == 0)
    def _():
        weight_copies[0].start()
        for copy in feature_copies(0):
            copy.start()
        for copy in weight_copies[1:]:
            copy.start()
        for i in range(1, steps):
            for copy in feature_copies(i):
                copy.start()

    for i in range(steps):

        @pl.when(step == i)
        def _(i=i):
            if i == 0:
                weight_copies[0].wait()
            for copy in feature_copies(i):
                copy.wait()

    def put_features(first, count):
        rows = feature_ref[pl.ds(first, count)]
        for b, copy in enumerate(side_copies(rows.astype(jnp.float32))):
            wide_ref[pl.ds(first, count), :, b * chan : (b + 1) * chan] = copy

    def encode(first, pairs):
        window = jnp.concatenate(
            [
                jnp.concatenate([wide_ref[first + 2 * k + a] for a in range(4)], axis=-1)
                for k in range(pairs)
            ]
        )
        both = jnp.dot(window, pair_w_ref[...], preferred_element_type=jnp.float32)
        both = jnp.maximum(both + enc_b, 0.0)
        cols = own_ref.shape[1]
        rows = []
        for d in range(2 * pairs):
            row = both[d // 2 * cols : (d // 2 + 1) * cols, d % 2 * chan : (d % 2 + 1) * chan]
            keep = jnp.logical_not((first + d == top) | (first + d == bottom))
            rows.append(jnp.where(keep, row, 0.0))
        for b, copy in enumerate(side_copies(jnp.stack(rows))):
            enc_ref[pl.ds(first, 2 * pairs), :, b * chan : (b + 1) * chan] = copy

    cols = own_ref.shape[1]
    row_blocks = cols // BLOCK
    pairs = source_ref.shape[0]
    peers = send_ref.shape[0]

    def send(n):
        start = pl.multiple_of(n // peers * 2 * BLOCK, 2 * BLOCK)
        place = send_ref.at[n % peers, pl.ds(start, 2 * BLOCK)]
        return pltpu.make_async_copy(all_ref.at[chosen_ref[n]], place, send_sem)

    def anchor(n):
        return pltpu.make_async_copy(all_ref.at[source_ref[n]], anchor_ref.at[n], anchor_sem)

    def ship(first, end):
        @pl.loop(0, chosen_ref.shape[0], unroll=4)
        def _(n):
            pl.when((chosen_ref[n] >= first) & (chosen_ref[n] < end))(lambda: send(n).start())

        @pl.loop(0, pairs, unroll=4)
        def _(n):
            pl.when((source_ref[n] >= first) & (source_ref[n] < end))(lambda: anchor(n).start())

    def fold_copies():
        return (
            pltpu.make_async_copy(
                send_fold_ref, send_ref.at[:, pl.ds(4 * BLOCK, FOLD_ROWS)], fold_sem.at[0]
            ),
            pltpu.make_async_copy(
                anchor_fold_ref, anchor_ref.at[pairs, pl.ds(0, pairs)], fold_sem.at[1]
            ),
        )

    @pl.when(step == 1)
    def _():
        stacked = jnp.concatenate(
            [fold_ref[:, c * BLOCK : (c + 1) * BLOCK] for c in range(row_blocks)]
        ).astype(jnp.float32)
        order = lax.broadcasted_iota(jnp.int32, (stacked.shape[0], 1), 0)
        block = lax.rem(order, fold_ref.shape[0]) * row_blocks + order // fold_ref.shape[0]

        def picked(row):
            return lax.dot_general(
                (block == row).astype(jnp.float32), stacked, (((0,), (0,)), ((), ())),
                preferred_element_type=jnp.float32,
            )

        rows = picked(chosen_row_ref[...])
        place = lax.broadcasted_iota(jnp.int32, send_fold_ref.shape, 1)
        both = jnp.where(place == 0, rows[:peers][:, None], rows[peers:][:, None])
        send_fold_ref[...] = both.astype(jnp.bfloat16)
        anchor_fold_ref[...] = picked(source_row_ref[...]).astype(jnp.bfloat16)
        for copy in fold_copies():
            copy.start()

    @pl.when(step == 0)
    def _():
        for p in range(4):
            for b in range(3):
                k = pl.ds((p * 3 + b) * chan, chan)
                zero = jnp.zeros((chan, chan), jnp.bfloat16)
                pair_w_ref[k, 0:chan] = enc_w_ref[p, b] if p < 3 else zero
                pair_w_ref[k, chan : 2 * chan] = enc_w_ref[p - 1, b] if p > 0 else zero
        put_features(0, 4)
        encode(0, 1)

    base = step * ROWS_STEP
    put_features(base + 4, ROWS_STEP)

    for d in range(0, ROWS_STEP, 2 * ENC_PAIRS):
        encode(base + 2 + d, ENC_PAIRS)

    @pl.when(step == 0)
    def _():
        for copy in weight_copies[1:]:
            copy.wait()

    for r in range(0, ROWS_STEP, DOT_ROWS):
        parts = [enc_ref[pl.ds(base + r + a, DOT_ROWS)] for a in range(3)]
        window = jnp.concatenate([v.reshape(DOT_ROWS * cols, 3 * chan) for v in parts], axis=-1)
        hidden = jnp.dot(window, head_w_ref[...], preferred_element_type=jnp.float32)
        hidden = jnp.maximum(hidden + head_b_ref[...], 0.0).astype(jnp.bfloat16)
        raw = jnp.dot(hidden, final_w_ref[...], preferred_element_type=jnp.float32)
        raw = raw + final_b_ref[...]
        norm = jnp.sum(raw * raw, axis=-1, keepdims=True)
        unit = (raw * lax.rsqrt(norm + 1e-06)).astype(jnp.bfloat16)
        place = pl.ds((base + r) * row_blocks, DOT_ROWS * row_blocks)
        for h in range(2):
            all_ref[place, h * BLOCK : (h + 1) * BLOCK] = unit[:, h * LANES : (h + 1) * LANES].reshape(
                DOT_ROWS * row_blocks, BLOCK, LANES
            )
    done = pl.ds(base * row_blocks, ROWS_STEP * row_blocks)
    for h in range(2):
        pltpu.make_async_copy(
            all_ref.at[done, pl.ds(h * BLOCK, BLOCK)],
            out_ref.at[done, :, pl.ds(h * LANES, LANES)],
            out_sem,
        ).start()

    @pl.when(step == last)
    def _():
        ship(0, all_ref.shape[0])

        @pl.loop(0, chosen_ref.shape[0], unroll=4)
        def _(n):
            pl.when(chosen_ref[n] >= 0)(lambda: send(n).wait())

        every = anchor_ref.at[pl.ds(0, source_ref.shape[0])]
        pltpu.make_async_copy(every, every, anchor_sem).wait()
        for copy in fold_copies():
            copy.wait()
        pltpu.make_async_copy(all_ref, all_ref, out_sem).wait()


def describe(
    chosen, source, folds, low, own, high, enc_w, enc_b, head_w, head_b, final_w, final_b
):
    rows, cols, chan = own.shape
    desc = final_w.shape[1]
    count = rows * cols // BLOCK
    whole = pl.BlockSpec(memory_space=pltpu.VMEM)
    scalars = pl.BlockSpec(memory_space=pltpu.SMEM)
    anywhere = pl.BlockSpec(memory_space=pl.ANY)
    macs = rows * cols * (12 * chan * chan + 9 * chan * desc + desc * desc)

    def half_lanes(n, height):
        return jax.ShapeDtypeStruct((n, height, LANES), jnp.bfloat16)

    return pl.pallas_call(
        describe_kernel,
        grid=(rows // ROWS_STEP,),
        in_specs=[scalars] * 2
        + [whole] * 3
        + [anywhere] * 4
        + [whole, anywhere, whole, anywhere, whole],
        out_specs=[pl.BlockSpec(memory_space=pl.ANY)] * 3,
        out_shape=[
            jax.ShapeDtypeStruct((count, BLOCK, desc), jnp.bfloat16),
            half_lanes(chosen.shape[0] // 2, 4 * BLOCK + FOLD_ROWS),
            half_lanes(source.shape[0] + 1, 2 * BLOCK),
        ],
        scratch_shapes=[
            pltpu.VMEM((rows + 4, cols, chan), jnp.bfloat16),
            pltpu.VMEM(enc_w.shape, jnp.bfloat16),
            pltpu.VMEM((9 * chan, desc), jnp.bfloat16),
            pltpu.VMEM(final_w.shape, jnp.bfloat16),
            pltpu.SemaphoreType.DMA((2 * (rows // ROWS_STEP),)),
            pltpu.SemaphoreType.DMA((3,)),
            pltpu.VMEM((rows + 4, cols, 3 * chan), jnp.bfloat16),
            pltpu.VMEM((rows + 2, cols, 3 * chan), jnp.bfloat16),
            pltpu.VMEM((12 * chan, 2 * chan), jnp.bfloat16),
            pltpu.VMEM((count, 2 * BLOCK, LANES), jnp.bfloat16),
            pltpu.VMEM((chosen.shape[0] // 2, FOLD_ROWS, LANES), jnp.bfloat16),
            pltpu.VMEM((source.shape[0], BLOCK), jnp.bfloat16),
            pltpu.SemaphoreType.DMA,
            pltpu.SemaphoreType.DMA,
            pltpu.SemaphoreType.DMA,
            pltpu.SemaphoreType.DMA((2,)),
        ],
        compiler_params=pltpu.CompilerParams(vmem_limit_bytes=56 * 2**20),
        cost_estimate=pl.CostEstimate(
            flops=2 * macs, bytes_accessed=rows * cols * (chan + desc) * 2, transcendentals=rows * cols
        ),
    )(
        chosen, source, chosen[None], source[None], folds, low, own, high, enc_w, enc_b[None], head_w.reshape(-1, desc),
        head_b[None], final_w, final_b[None],
    )


def match_kernel(
    slot_ref, anchors_ref, arrived_ref, out_ref, anchor_ref, partner_ref, anchor_fold_ref,
    partner_fold_ref, anchor_sem, partner_sem, fold_sem,
):
    groups = out_ref.shape[0] // PAIRS_STEP

    def products(left, right):
        return SCORE_SCALE * LOG2_E * lax.dot_general(
            left, right, (((1,), (1,)), ((), ())), preferred_element_type=jnp.float32
        )

    def relative_cost(folds):
        least = jnp.min(folds, axis=1, keepdims=True)
        return FOLD_PENALTY * LOG2_E * (folds - least)

    def group(g):
        return pl.ds(g * PAIRS_STEP, PAIRS_STEP)

    def anchors(g):
        return pltpu.make_async_copy(
            anchors_ref.at[group(g)], anchor_ref.at[group(g)], anchor_sem.at[g]
        )

    pairs = out_ref.shape[0]
    fold_copies = (
        pltpu.make_async_copy(
            arrived_ref.at[:, pl.ds(4 * BLOCK, FOLD_ROWS)], partner_fold_ref, fold_sem.at[0]
        ),
        pltpu.make_async_copy(
            anchors_ref.at[pairs, pl.ds(0, pairs)], anchor_fold_ref, fold_sem.at[1]
        ),
    )
    for copy in fold_copies:
        copy.start()

    def place(pair):
        return slot_ref[pair] // 2, pl.multiple_of(slot_ref[pair] % 2 * 2 * BLOCK, 2 * BLOCK)

    @pl.loop(0, groups)
    def _(g):
        anchors(g).start()
        for n in range(PAIRS_STEP):
            pair = g * PAIRS_STEP + n
            owner, start = place(pair)
            pltpu.make_async_copy(
                arrived_ref.at[owner, pl.ds(start, 2 * BLOCK)], partner_ref.at[pair], partner_sem.at[g]
            ).start()

    for copy in fold_copies:
        copy.wait()

    @pl.loop(0, groups)
    def _(g):
        anchor_cost = relative_cost(anchor_fold_ref[group(g)].astype(jnp.float32))
        anchor_column = jnp.transpose(anchor_cost)
        partner_fold = []
        for n in range(PAIRS_STEP):
            owner, start = place(g * PAIRS_STEP + n)
            both = partner_fold_ref[owner].astype(jnp.float32)
            partner_fold.append(jnp.where(start == 0, both[0:1], both[1:2]))
        partner_column = jnp.transpose(relative_cost(jnp.concatenate(partner_fold)))
        anchors(g).wait()
        here = partner_ref.at[group(g)]
        pltpu.make_async_copy(here, here, partner_sem.at[g]).wait()
        left, right = [
            [
                jnp.concatenate([ref[g * PAIRS_STEP + n, h * BLOCK : (h + 1) * BLOCK] for h in range(2)], axis=1)
                for n in range(PAIRS_STEP)
            ]
            for ref in (anchor_ref, partner_ref)
        ]

        over_i = []
        for n in range(PAIRS_STEP):
            by_i = products(left[n], right[n]) - anchor_column[:, n : n + 1]
            over_i.append(jnp.log2(jnp.sum(jnp.exp2(by_i), axis=0, keepdims=True)))
        over_i = jnp.transpose(jnp.concatenate(over_i))
        result = []
        for n in range(PAIRS_STEP):
            plain = products(right[n], left[n])
            by_j = plain - partner_column[:, n : n + 1]
            total = jnp.sum(jnp.exp2(by_j), axis=0, keepdims=True)
            best = jnp.max(by_j + (plain - over_i[:, n : n + 1]), axis=0, keepdims=True)
            result.append(jnp.exp2(best - anchor_cost[n : n + 1]) / total)
        out_ref[group(g)] = jnp.concatenate(result)


def match(slot, anchors, arrived):
    pairs = slot.shape[0]
    return pl.pallas_call(
        match_kernel,
        in_specs=[pl.BlockSpec(memory_space=pltpu.SMEM)] + [pl.BlockSpec(memory_space=pl.ANY)] * 2,
        out_specs=pl.BlockSpec(memory_space=pltpu.VMEM),
        out_shape=jax.ShapeDtypeStruct((pairs, BLOCK), jnp.float32),
        scratch_shapes=[pltpu.VMEM((pairs, 2 * BLOCK, LANES), jnp.bfloat16)] * 2
        + [
            pltpu.VMEM((pairs, BLOCK), jnp.bfloat16),
            pltpu.VMEM((arrived.shape[0], FOLD_ROWS, LANES), jnp.bfloat16),
        ]
        + [pltpu.SemaphoreType.DMA((pairs // PAIRS_STEP,))] * 2
        + [pltpu.SemaphoreType.DMA((2,))],
        compiler_params=pltpu.CompilerParams(vmem_limit_bytes=VMEM_MATCH),
    )(slot, anchors, arrived)


def local(
    features, fold_mask, encoder_weight, encoder_bias, head_weight, head_bias,
    final_weight, final_bias, pair_source, pair_target,
):
    own_band = features[0]
    band_rows, band_cols, _ = own_band.shape
    tile_count = lax.axis_size("tile")
    tile_here = lax.axis_index("tile")
    section = lax.axis_index("sec")
    swap = [(0, 1), (1, 0)]
    down = [(i, i + 1) for i in range(tile_count - 1)]
    up = [(j, i) for i, j in down]
    low = lax.ppermute(own_band[-2:], "tile", down)
    high = lax.ppermute(own_band[:2], "tile", up)

    block_count = band_rows * band_cols // BLOCK
    pair_count = pair_source.shape[1]
    capacity = 2
    wanted = lax.dynamic_index_in_dim(pair_target, 1 - section, 0, keepdims=False).reshape(
        tile_count, pair_count
    )
    matched = (wanted // block_count == tile_here).astype(jnp.int32)
    order_rank = jnp.cumsum(matched, axis=1) - matched
    slot_hot = matched[None] * (
        order_rank[None] == jnp.arange(capacity)[:, None, None]
    ).astype(jnp.int32)
    chosen = jnp.sum(slot_hot * (wanted % block_count + 1)[None], axis=2) - 1
    targets = lax.dynamic_index_in_dim(wanted, tile_here, 0, keepdims=False)
    owners = targets // block_count
    earlier = jnp.arange(pair_count)[None, :] < jnp.arange(pair_count)[:, None]
    slot_rank = jnp.sum(((owners[None, :] == owners[:, None]) & earlier).astype(jnp.int32), axis=1)
    slot_index = owners * capacity + slot_rank

    described, send_blocks, anchors = describe(
        chosen.reshape(-1), pair_source[0], fold_mask[0], low, own_band, high, encoder_weight,
        encoder_bias, head_weight, head_bias, final_weight, final_bias,
    )
    sibling_anchors = lax.ppermute(anchors, "sec", swap)
    send_blocks, sibling_anchors, slot_index = lax.optimization_barrier(
        (send_blocks, sibling_anchors, slot_index)
    )
    arrived = lax.all_to_all(send_blocks, "tile", split_axis=0, concat_axis=0, tiled=True)
    confidence = match(slot_index, sibling_anchors, arrived)
    confidence = lax.ppermute(confidence, "sec", swap)
    return (described.reshape(1, band_rows, band_cols, -1), confidence[None])


def solution(mesh):
    return jax.shard_map(
        local,
        mesh=mesh,
        in_specs=(
            P("sec", "tile", None, None), P("sec", "tile", None), P(), P(), P(), P(), P(), P(),
            P("sec", "tile"), P(),
        ),
        out_specs=(P("sec", "tile", None, None), P("sec", "tile", None)),
        check_vma=False,
    )
```

```python
import functools

import jax
import jax.numpy as jnp
from jax import lax
from jax.experimental import pallas as pl
from jax.experimental.pallas import tpu as pltpu
from jax.sharding import PartitionSpec as P

BLOCK = 128
SCORE_SCALE = 10.0
FOLD_PENALTY = 200.0
LOG2_E = 1.4426950408889634
ROWS_STEP = 8
FOLD_ROWS = 16
LANES = 128
ENC_PAIRS = 1
DOT_ROWS = 8
PAIRS_STEP = 32
VMEM_MATCH = 56 * 2**20


def side_copies(rows):
    cols = rows.shape[1]
    flat = rows.reshape(rows.shape[0] * cols, rows.shape[2])
    column = lax.broadcasted_iota(jnp.int32, rows.shape, 1).reshape(flat.shape)
    before = jnp.where(column == 0, 0.0, pltpu.roll(flat, 1, 0))
    after = jnp.where(column == cols - 1, 0.0, pltpu.roll(flat, flat.shape[0] - 1, 0))
    return [v.reshape(rows.shape).astype(jnp.bfloat16) for v in (before, flat, after)]


def describe_kernel(
    chosen_ref, source_ref, chosen_row_ref, source_row_ref, fold_ref, low_ref, own_ref, high_ref,
    enc_w_hbm, enc_b_ref, head_w_hbm, head_b_ref, final_w_hbm, final_b_ref, out_ref, send_ref,
    anchor_ref, feature_ref, enc_w_ref, head_w_ref, final_w_ref, in_sem, weight_sem, wide_ref,
    enc_ref, pair_w_ref, all_ref, send_fold_ref, anchor_fold_ref, out_sem, send_sem, anchor_sem,
    fold_sem,
):
    step = pl.program_id(0)
    last = pl.num_programs(0) - 1
    chan = own_ref.shape[2]
    height = own_ref.shape[0]
    steps = height // ROWS_STEP
    tile_here = lax.axis_index("tile")
    top = jnp.where(tile_here == 0, 0, -1)
    bottom = jnp.where(tile_here == lax.axis_size("tile") - 1, enc_ref.shape[0] - 1, -1)
    enc_b = jnp.concatenate([enc_b_ref[...]] * 2, axis=-1)

    def feature_copies(i):
        first = 0 if i == 0 else i * ROWS_STEP + 2
        end = min((i + 1) * ROWS_STEP + 2, height)
        parts = [(own_ref.at[pl.ds(first, end - first)], first + 2)]
        if i == 0:
            parts.append((low_ref, 0))
        if i == steps - 1:
            parts.append((high_ref, height + 2))
        return [
            pltpu.make_async_copy(
                part, feature_ref.at[pl.ds(place, part.shape[0])], in_sem.at[2 * i + n]
            )
            for n, (part, place) in enumerate(parts)
        ]

    weight_copies = [
        pltpu.make_async_copy(source, place, weight_sem.at[n])
        for n, (source, place) in enumerate(
            ((enc_w_hbm, enc_w_ref), (head_w_hbm, head_w_ref), (final_w_hbm, final_w_ref))
        )
    ]

    @pl.when(step == 0)
    def _():
        weight_copies[0].start()
        for copy in feature_copies(0):
            copy.start()
        for copy in weight_copies[1:]:
            copy.start()
        for i in range(1, steps):
            for copy in feature_copies(i):
                copy.start()

    for i in range(steps):

        @pl.when(step == i)
        def _(i=i):
            if i == 0:
                weight_copies[0].wait()
            for copy in feature_copies(i):
                copy.wait()

    def put_features(first, count):
        rows = feature_ref[pl.ds(first, count)]
        for b, copy in enumerate(side_copies(rows.astype(jnp.float32))):
            wide_ref[pl.ds(first, count), :, b * chan : (b + 1) * chan] = copy

    def encode(first, pairs):
        window = jnp.concatenate(
            [
                jnp.concatenate([wide_ref[first + 2 * k + a] for a in range(4)], axis=-1)
                for k in range(pairs)
            ]
        )
        both = jnp.dot(window, pair_w_ref[...], preferred_element_type=jnp.float32)
        both = jnp.maximum(both + enc_b, 0.0)
        cols = own_ref.shape[1]
        rows = []
        for d in range(2 * pairs):
            row = both[d // 2 * cols : (d // 2 + 1) * cols, d % 2 * chan : (d % 2 + 1) * chan]
            keep = jnp.logical_not((first + d == top) | (first + d == bottom))
            rows.append(jnp.where(keep, row, 0.0))
        for b, copy in enumerate(side_copies(jnp.stack(rows))):
            enc_ref[pl.ds(first, 2 * pairs), :, b * chan : (b + 1) * chan] = copy

    cols = own_ref.shape[1]
    row_blocks = cols // BLOCK
    pairs = source_ref.shape[0]
    peers = send_ref.shape[0]

    def send(n):
        start = pl.multiple_of(n // peers * 2 * BLOCK, 2 * BLOCK)
        place = send_ref.at[n % peers, pl.ds(start, 2 * BLOCK)]
        return pltpu.make_async_copy(all_ref.at[chosen_ref[n]], place, send_sem)

    def anchor(n):
        return pltpu.make_async_copy(all_ref.at[source_ref[n]], anchor_ref.at[n], anchor_sem)

    def ship(first, end):
        @pl.loop(0, chosen_ref.shape[0], unroll=4)
        def _(n):
            pl.when((chosen_ref[n] >= first) & (chosen_ref[n] < end))(lambda: send(n).start())

        @pl.loop(0, pairs, unroll=4)
        def _(n):
            pl.when((source_ref[n] >= first) & (source_ref[n] < end))(lambda: anchor(n).start())

    def fold_copies():
        return (
            pltpu.make_async_copy(
                send_fold_ref, send_ref.at[:, pl.ds(4 * BLOCK, FOLD_ROWS)], fold_sem.at[0]
            ),
            pltpu.make_async_copy(
                anchor_fold_ref, anchor_ref.at[pairs, pl.ds(0, pairs)], fold_sem.at[1]
            ),
        )

    @pl.when(step == 1)
    def _():
        stacked = jnp.concatenate(
            [fold_ref[:, c * BLOCK : (c + 1) * BLOCK] for c in range(row_blocks)]
        ).astype(jnp.float32)
        order = lax.broadcasted_iota(jnp.int32, (stacked.shape[0], 1), 0)
        block = lax.rem(order, fold_ref.shape[0]) * row_blocks + order // fold_ref.shape[0]

        def picked(row):
            return lax.dot_general(
                (block == row).astype(jnp.float32), stacked, (((0,), (0,)), ((), ())),
                preferred_element_type=jnp.float32,
            )

        rows = picked(chosen_row_ref[...])
        place = lax.broadcasted_iota(jnp.int32, send_fold_ref.shape, 1)
        both = jnp.where(place == 0, rows[:peers][:, None], rows[peers:][:, None])
        send_fold_ref[...] = both.astype(jnp.bfloat16)
        anchor_fold_ref[...] = picked(source_row_ref[...]).astype(jnp.bfloat16)
        for copy in fold_copies():
            copy.start()

    @pl.when(step == 0)
    def _():
        for p in range(4):
            for b in range(3):
                k = pl.ds((p * 3 + b) * chan, chan)
                zero = jnp.zeros((chan, chan), jnp.bfloat16)
                pair_w_ref[k, 0:chan] = enc_w_ref[p, b] if p < 3 else zero
                pair_w_ref[k, chan : 2 * chan] = enc_w_ref[p - 1, b] if p > 0 else zero
        put_features(0, 4)
        encode(0, 1)

    base = step * ROWS_STEP
    put_features(base + 4, ROWS_STEP)

    for d in range(0, ROWS_STEP, 2 * ENC_PAIRS):
        encode(base + 2 + d, ENC_PAIRS)

    @pl.when(step == 0)
    def _():
        for copy in weight_copies[1:]:
            copy.wait()

    for r in range(0, ROWS_STEP, DOT_ROWS):
        parts = [enc_ref[pl.ds(base + r + a, DOT_ROWS)] for a in range(3)]
        window = jnp.concatenate([v.reshape(DOT_ROWS * cols, 3 * chan) for v in parts], axis=-1)
        hidden = jnp.dot(window, head_w_ref[...], preferred_element_type=jnp.float32)
        hidden = jnp.maximum(hidden + head_b_ref[...], 0.0).astype(jnp.bfloat16)
        raw = jnp.dot(hidden, final_w_ref[...], preferred_element_type=jnp.float32)
        raw = raw + final_b_ref[...]
        norm = jnp.sum(raw * raw, axis=-1, keepdims=True)
        unit = (raw * lax.rsqrt(norm + 1e-06)).astype(jnp.bfloat16)
        place = pl.ds((base + r) * row_blocks, DOT_ROWS * row_blocks)
        for h in range(2):
            all_ref[place, h * BLOCK : (h + 1) * BLOCK] = unit[:, h * LANES : (h + 1) * LANES].reshape(
                DOT_ROWS * row_blocks, BLOCK, LANES
            )
    done = pl.ds(base * row_blocks, ROWS_STEP * row_blocks)
    for h in range(2):
        pltpu.make_async_copy(
            all_ref.at[done, pl.ds(h * BLOCK, BLOCK)],
            out_ref.at[done, :, pl.ds(h * LANES, LANES)],
            out_sem,
        ).start()

    @pl.when(step == last)
    def _():
        ship(0, all_ref.shape[0])

        @pl.loop(0, chosen_ref.shape[0], unroll=4)
        def _(n):
            pl.when(chosen_ref[n] >= 0)(lambda: send(n).wait())

        every = anchor_ref.at[pl.ds(0, source_ref.shape[0])]
        pltpu.make_async_copy(every, every, anchor_sem).wait()
        for copy in fold_copies():
            copy.wait()
        pltpu.make_async_copy(all_ref, all_ref, out_sem).wait()


def describe(
    chosen, source, folds, low, own, high, enc_w, enc_b, head_w, head_b, final_w, final_b
):
    rows, cols, chan = own.shape
    desc = final_w.shape[1]
    count = rows * cols // BLOCK
    whole = pl.BlockSpec(memory_space=pltpu.VMEM)
    scalars = pl.BlockSpec(memory_space=pltpu.SMEM)
    anywhere = pl.BlockSpec(memory_space=pl.ANY)
    macs = rows * cols * (12 * chan * chan + 9 * chan * desc + desc * desc)

    def half_lanes(n, height):
        return jax.ShapeDtypeStruct((n, height, LANES), jnp.bfloat16)

    return pl.pallas_call(
        describe_kernel,
        grid=(rows // ROWS_STEP,),
        in_specs=[scalars] * 2
        + [whole] * 3
        + [anywhere] * 4
        + [whole, anywhere, whole, anywhere, whole],
        out_specs=[pl.BlockSpec(memory_space=pl.ANY)] * 3,
        out_shape=[
            jax.ShapeDtypeStruct((count, BLOCK, desc), jnp.bfloat16),
            half_lanes(chosen.shape[0] // 2, 4 * BLOCK + FOLD_ROWS),
            half_lanes(source.shape[0] + 1, 2 * BLOCK),
        ],
        scratch_shapes=[
            pltpu.VMEM((rows + 4, cols, chan), jnp.bfloat16),
            pltpu.VMEM(enc_w.shape, jnp.bfloat16),
            pltpu.VMEM((9 * chan, desc), jnp.bfloat16),
            pltpu.VMEM(final_w.shape, jnp.bfloat16),
            pltpu.SemaphoreType.DMA((2 * (rows // ROWS_STEP),)),
            pltpu.SemaphoreType.DMA((3,)),
            pltpu.VMEM((rows + 4, cols, 3 * chan), jnp.bfloat16),
            pltpu.VMEM((rows + 2, cols, 3 * chan), jnp.bfloat16),
            pltpu.VMEM((12 * chan, 2 * chan), jnp.bfloat16),
            pltpu.VMEM((count, 2 * BLOCK, LANES), jnp.bfloat16),
            pltpu.VMEM((chosen.shape[0] // 2, FOLD_ROWS, LANES), jnp.bfloat16),
            pltpu.VMEM((source.shape[0], BLOCK), jnp.bfloat16),
            pltpu.SemaphoreType.DMA,
            pltpu.SemaphoreType.DMA,
            pltpu.SemaphoreType.DMA,
            pltpu.SemaphoreType.DMA((2,)),
        ],
        compiler_params=pltpu.CompilerParams(vmem_limit_bytes=56 * 2**20),
        cost_estimate=pl.CostEstimate(
            flops=2 * macs, bytes_accessed=rows * cols * (chan + desc) * 2, transcendentals=rows * cols
        ),
    )(
        chosen, source, chosen[None], source[None], folds, low, own, high, enc_w, enc_b[None], head_w.reshape(-1, desc),
        head_b[None], final_w, final_b[None],
    )


def match_kernel(
    slot_ref, anchors_ref, arrived_ref, out_ref, anchor_ref, partner_ref, anchor_fold_ref,
    partner_fold_ref, anchor_sem, partner_sem, fold_sem,
):
    groups = out_ref.shape[0] // PAIRS_STEP

    def products(left, right):
        return SCORE_SCALE * LOG2_E * lax.dot_general(
            left, right, (((1,), (1,)), ((), ())), preferred_element_type=jnp.float32
        )

    def relative_cost(folds):
        least = jnp.min(folds, axis=1, keepdims=True)
        return FOLD_PENALTY * LOG2_E * (folds - least)

    def group(g):
        return pl.ds(g * PAIRS_STEP, PAIRS_STEP)

    def anchors(g):
        return pltpu.make_async_copy(
            anchors_ref.at[group(g)], anchor_ref.at[group(g)], anchor_sem.at[g]
        )

    pairs = out_ref.shape[0]
    fold_copies = (
        pltpu.make_async_copy(
            arrived_ref.at[:, pl.ds(4 * BLOCK, FOLD_ROWS)], partner_fold_ref, fold_sem.at[0]
        ),
        pltpu.make_async_copy(
            anchors_ref.at[pairs, pl.ds(0, pairs)], anchor_fold_ref, fold_sem.at[1]
        ),
    )
    for copy in fold_copies:
        copy.start()

    def place(pair):
        return slot_ref[pair] // 2, pl.multiple_of(slot_ref[pair] % 2 * 2 * BLOCK, 2 * BLOCK)

    @pl.loop(0, groups)
    def _(g):
        anchors(g).start()
        for n in range(PAIRS_STEP):
            pair = g * PAIRS_STEP + n
            owner, start = place(pair)
            pltpu.make_async_copy(
                arrived_ref.at[owner, pl.ds(start, 2 * BLOCK)], partner_ref.at[pair], partner_sem.at[g]
            ).start()

    for copy in fold_copies:
        copy.wait()

    @pl.loop(0, groups)
    def _(g):
        anchor_cost = relative_cost(anchor_fold_ref[group(g)].astype(jnp.float32))
        anchor_column = jnp.transpose(anchor_cost)
        partner_fold = []
        for n in range(PAIRS_STEP):
            owner, start = place(g * PAIRS_STEP + n)
            both = partner_fold_ref[owner].astype(jnp.float32)
            partner_fold.append(jnp.where(start == 0, both[0:1], both[1:2]))
        partner_column = jnp.transpose(relative_cost(jnp.concatenate(partner_fold)))
        anchors(g).wait()
        here = partner_ref.at[group(g)]
        pltpu.make_async_copy(here, here, partner_sem.at[g]).wait()
        left, right = [
            [
                jnp.concatenate([ref[g * PAIRS_STEP + n, h * BLOCK : (h + 1) * BLOCK] for h in range(2)], axis=1)
                for n in range(PAIRS_STEP)
            ]
            for ref in (anchor_ref, partner_ref)
        ]

        over_i = []
        for n in range(PAIRS_STEP):
            by_i = products(left[n], right[n]) - anchor_column[:, n : n + 1]
            over_i.append(jnp.log2(jnp.sum(jnp.exp2(by_i), axis=0, keepdims=True)))
        over_i = jnp.transpose(jnp.concatenate(over_i))
        result = []
        for n in range(PAIRS_STEP):
            plain = products(right[n], left[n])
            by_j = plain - partner_column[:, n : n + 1]
            total = jnp.sum(jnp.exp2(by_j), axis=0, keepdims=True)
            best = jnp.max(by_j + (plain - over_i[:, n : n + 1]), axis=0, keepdims=True)
            result.append(jnp.exp2(best - anchor_cost[n : n + 1]) / total)
        out_ref[group(g)] = jnp.concatenate(result)


def match(slot, anchors, arrived):
    pairs = slot.shape[0]
    return pl.pallas_call(
        match_kernel,
        in_specs=[pl.BlockSpec(memory_space=pltpu.SMEM)] + [pl.BlockSpec(memory_space=pl.ANY)] * 2,
        out_specs=pl.BlockSpec(memory_space=pltpu.VMEM),
        out_shape=jax.ShapeDtypeStruct((pairs, BLOCK), jnp.float32),
        scratch_shapes=[pltpu.VMEM((pairs, 2 * BLOCK, LANES), jnp.bfloat16)] * 2
        + [
            pltpu.VMEM((pairs, BLOCK), jnp.bfloat16),
            pltpu.VMEM((arrived.shape[0], FOLD_ROWS, LANES), jnp.bfloat16),
        ]
        + [pltpu.SemaphoreType.DMA((pairs // PAIRS_STEP,))] * 2
        + [pltpu.SemaphoreType.DMA((2,))],
        compiler_params=pltpu.CompilerParams(vmem_limit_bytes=VMEM_MATCH),
    )(slot, anchors, arrived)


def local(
    features, fold_mask, encoder_weight, encoder_bias, head_weight, head_bias,
    final_weight, final_bias, pair_source, pair_target,
):
    own_band = features[0]
    band_rows, band_cols, _ = own_band.shape
    tile_count = lax.axis_size("tile")
    tile_here = lax.axis_index("tile")
    section = lax.axis_index("sec")
    swap = [(0, 1), (1, 0)]
    down = [(i, i + 1) for i in range(tile_count - 1)]
    up = [(j, i) for i, j in down]
    low = lax.ppermute(own_band[-2:], "tile", down)
    high = lax.ppermute(own_band[:2], "tile", up)

    block_count = band_rows * band_cols // BLOCK
    pair_count = pair_source.shape[1]
    capacity = 2
    wanted = lax.dynamic_index_in_dim(pair_target, 1 - section, 0, keepdims=False).reshape(
        tile_count, pair_count
    )
    matched = wanted // block_count == tile_here
    within = wanted % block_count
    lower = jnp.min(jnp.where(matched, within, block_count), axis=1)
    upper = jnp.max(jnp.where(matched, within, -1), axis=1)
    chosen = jnp.stack([jnp.where(upper >= 0, lower, -1), jnp.where(upper > lower, upper, -1)])
    targets = lax.dynamic_index_in_dim(wanted, tile_here, 0, keepdims=False)
    owners = targets // block_count
    lower_named = (owners[None, :] == owners[:, None]) & (targets[None, :] < targets[:, None])
    slot_rank = jnp.any(lower_named, axis=1).astype(jnp.int32)
    slot_index = owners * capacity + slot_rank

    described, send_blocks, anchors = describe(
        chosen.reshape(-1), pair_source[0], fold_mask[0], low, own_band, high, encoder_weight,
        encoder_bias, head_weight, head_bias, final_weight, final_bias,
    )
    sibling_anchors = lax.ppermute(anchors, "sec", swap)
    send_blocks, sibling_anchors, slot_index = lax.optimization_barrier(
        (send_blocks, sibling_anchors, slot_index)
    )
    arrived = lax.all_to_all(send_blocks, "tile", split_axis=0, concat_axis=0, tiled=True)
    confidence = match(slot_index, sibling_anchors, arrived)
    confidence = lax.ppermute(confidence, "sec", swap)
    return (described.reshape(1, band_rows, band_cols, -1), confidence[None])


def solution(mesh):
    return jax.shard_map(
        local,
        mesh=mesh,
        in_specs=(
            P("sec", "tile", None, None), P("sec", "tile", None), P(), P(), P(), P(), P(), P(),
            P("sec", "tile"), P(),
        ),
        out_specs=(P("sec", "tile", None, None), P("sec", "tile", None)),
        check_vma=False,
    )
```

```python
import functools

import jax
import jax.numpy as jnp
from jax import lax
from jax.experimental import pallas as pl
from jax.experimental.pallas import tpu as pltpu
from jax.sharding import PartitionSpec as P

BLOCK = 128
SCORE_SCALE = 10.0
FOLD_PENALTY = 200.0
LOG2_E = 1.4426950408889634
ROWS_STEP = 8
FOLD_ROWS = 16
LANES = 128
ENC_PAIRS = 1
DOT_ROWS = 8
PAIRS_STEP = 32
VMEM_MATCH = 56 * 2**20


def side_copies(rows):
    cols = rows.shape[1]
    flat = rows.reshape(rows.shape[0] * cols, rows.shape[2])
    column = lax.broadcasted_iota(jnp.int32, rows.shape, 1).reshape(flat.shape)
    before = jnp.where(column == 0, 0.0, pltpu.roll(flat, 1, 0))
    after = jnp.where(column == cols - 1, 0.0, pltpu.roll(flat, flat.shape[0] - 1, 0))
    return [v.reshape(rows.shape).astype(jnp.bfloat16) for v in (before, flat, after)]


def describe_kernel(
    chosen_ref, source_ref, chosen_row_ref, source_row_ref, fold_ref, low_ref, own_ref, high_ref,
    enc_w_hbm, enc_b_ref, head_w_hbm, head_b_ref, final_w_hbm, final_b_ref, out_ref, send_ref,
    anchor_ref, feature_ref, enc_w_ref, head_w_ref, final_w_ref, in_sem, weight_sem, wide_ref,
    enc_ref, pair_w_ref, all_ref, send_fold_ref, anchor_fold_ref, out_sem, send_sem, anchor_sem,
    fold_sem,
):
    step = pl.program_id(0)
    last = pl.num_programs(0) - 1
    chan = own_ref.shape[2]
    height = own_ref.shape[0]
    steps = height // ROWS_STEP
    tile_here = lax.axis_index("tile")
    top = jnp.where(tile_here == 0, 0, -1)
    bottom = jnp.where(tile_here == lax.axis_size("tile") - 1, enc_ref.shape[0] - 1, -1)
    enc_b = jnp.concatenate([enc_b_ref[...]] * 2, axis=-1)

    def feature_copies(i):
        first = 0 if i == 0 else i * ROWS_STEP + 2
        end = min((i + 1) * ROWS_STEP + 2, height)
        parts = [(own_ref.at[pl.ds(first, end - first)], first + 2)]
        if i == 0:
            parts.append((low_ref, 0))
        if i == steps - 1:
            parts.append((high_ref, height + 2))
        return [
            pltpu.make_async_copy(
                part, feature_ref.at[pl.ds(place, part.shape[0])], in_sem.at[2 * i + n]
            )
            for n, (part, place) in enumerate(parts)
        ]

    weight_copies = [
        pltpu.make_async_copy(source, place, weight_sem.at[n])
        for n, (source, place) in enumerate(
            ((enc_w_hbm, enc_w_ref), (head_w_hbm, head_w_ref), (final_w_hbm, final_w_ref))
        )
    ]

    @pl.when(step == 0)
    def _():
        weight_copies[0].start()
        for copy in feature_copies(0):
            copy.start()
        for copy in weight_copies[1:]:
            copy.start()
        for i in range(1, steps):
            for copy in feature_copies(i):
                copy.start()

    for i in range(steps):

        @pl.when(step == i)
        def _(i=i):
            if i == 0:
                weight_copies[0].wait()
            for copy in feature_copies(i):
                copy.wait()

    def put_features(first, count):
        rows = feature_ref[pl.ds(first, count)]
        for b, copy in enumerate(side_copies(rows.astype(jnp.float32))):
            wide_ref[pl.ds(first, count), :, b * chan : (b + 1) * chan] = copy

    def encode(first, pairs):
        window = jnp.concatenate(
            [
                jnp.concatenate([wide_ref[first + 2 * k + a] for a in range(4)], axis=-1)
                for k in range(pairs)
            ]
        )
        both = jnp.dot(window, pair_w_ref[...], preferred_element_type=jnp.float32)
        both = jnp.maximum(both + enc_b, 0.0)
        cols = own_ref.shape[1]
        rows = []
        for d in range(2 * pairs):
            row = both[d // 2 * cols : (d // 2 + 1) * cols, d % 2 * chan : (d % 2 + 1) * chan]
            keep = jnp.logical_not((first + d == top) | (first + d == bottom))
            rows.append(jnp.where(keep, row, 0.0))
        for b, copy in enumerate(side_copies(jnp.stack(rows))):
            enc_ref[pl.ds(first, 2 * pairs), :, b * chan : (b + 1) * chan] = copy

    cols = own_ref.shape[1]
    row_blocks = cols // BLOCK
    pairs = source_ref.shape[0]
    peers = send_ref.shape[0]

    def send(n):
        start = pl.multiple_of(n // peers * 2 * BLOCK, 2 * BLOCK)
        place = send_ref.at[n % peers, pl.ds(start, 2 * BLOCK)]
        return pltpu.make_async_copy(all_ref.at[chosen_ref[n]], place, send_sem)

    def anchor(n):
        return pltpu.make_async_copy(all_ref.at[source_ref[n]], anchor_ref.at[n], anchor_sem)

    def ship_anchors(first, end):
        @pl.loop(0, pairs, unroll=4)
        def _(n):
            pl.when((source_ref[n] >= first) & (source_ref[n] < end))(lambda: anchor(n).start())

    @pl.when(step == last)
    def _():
        ship_anchors(0, step * ROWS_STEP * row_blocks)

    def fold_copies():
        return (
            pltpu.make_async_copy(
                send_fold_ref, send_ref.at[:, pl.ds(4 * BLOCK, FOLD_ROWS)], fold_sem.at[0]
            ),
            pltpu.make_async_copy(
                anchor_fold_ref, anchor_ref.at[pairs, pl.ds(0, pairs)], fold_sem.at[1]
            ),
        )

    @pl.when(step == 1)
    def _():
        stacked = jnp.concatenate(
            [fold_ref[:, c * BLOCK : (c + 1) * BLOCK] for c in range(row_blocks)]
        ).astype(jnp.float32)
        order = lax.broadcasted_iota(jnp.int32, (stacked.shape[0], 1), 0)
        block = lax.rem(order, fold_ref.shape[0]) * row_blocks + order // fold_ref.shape[0]

        def picked(row):
            return lax.dot_general(
                (block == row).astype(jnp.float32), stacked, (((0,), (0,)), ((), ())),
                preferred_element_type=jnp.float32,
            )

        rows = picked(chosen_row_ref[...])
        place = lax.broadcasted_iota(jnp.int32, send_fold_ref.shape, 1)
        both = jnp.where(place == 0, rows[:peers][:, None], rows[peers:][:, None])
        send_fold_ref[...] = both.astype(jnp.bfloat16)
        anchor_fold_ref[...] = picked(source_row_ref[...]).astype(jnp.bfloat16)
        for copy in fold_copies():
            copy.start()

    @pl.when(step == 0)
    def _():
        for p in range(4):
            for b in range(3):
                k = pl.ds((p * 3 + b) * chan, chan)
                zero = jnp.zeros((chan, chan), jnp.bfloat16)
                pair_w_ref[k, 0:chan] = enc_w_ref[p, b] if p < 3 else zero
                pair_w_ref[k, chan : 2 * chan] = enc_w_ref[p - 1, b] if p > 0 else zero
        put_features(0, 4)
        encode(0, 1)

    base = step * ROWS_STEP
    put_features(base + 4, ROWS_STEP)

    for d in range(0, ROWS_STEP, 2 * ENC_PAIRS):
        encode(base + 2 + d, ENC_PAIRS)

    @pl.when(step == 0)
    def _():
        for copy in weight_copies[1:]:
            copy.wait()

    for r in range(0, ROWS_STEP, DOT_ROWS):
        parts = [enc_ref[pl.ds(base + r + a, DOT_ROWS)] for a in range(3)]
        window = jnp.concatenate([v.reshape(DOT_ROWS * cols, 3 * chan) for v in parts], axis=-1)
        hidden = jnp.dot(window, head_w_ref[...], preferred_element_type=jnp.float32)
        hidden = jnp.maximum(hidden + head_b_ref[...], 0.0).astype(jnp.bfloat16)
        raw = jnp.dot(hidden, final_w_ref[...], preferred_element_type=jnp.float32)
        raw = raw + final_b_ref[...]
        norm = jnp.sum(raw * raw, axis=-1, keepdims=True)
        unit = (raw * lax.rsqrt(norm + 1e-06)).astype(jnp.bfloat16)
        place = pl.ds((base + r) * row_blocks, DOT_ROWS * row_blocks)
        for h in range(2):
            all_ref[place, h * BLOCK : (h + 1) * BLOCK] = unit[:, h * LANES : (h + 1) * LANES].reshape(
                DOT_ROWS * row_blocks, BLOCK, LANES
            )
    done = pl.ds(base * row_blocks, ROWS_STEP * row_blocks)
    for h in range(2):
        pltpu.make_async_copy(
            all_ref.at[done, pl.ds(h * BLOCK, BLOCK)],
            out_ref.at[done, :, pl.ds(h * LANES, LANES)],
            out_sem,
        ).start()

    @pl.when(step == last)
    def _():
        @pl.loop(0, chosen_ref.shape[0], unroll=4)
        def _(n):
            pl.when(chosen_ref[n] >= 0)(lambda: send(n).start())

        ship_anchors(base * row_blocks, all_ref.shape[0])

        @pl.loop(0, chosen_ref.shape[0], unroll=4)
        def _(n):
            pl.when(chosen_ref[n] >= 0)(lambda: send(n).wait())

        every = anchor_ref.at[pl.ds(0, source_ref.shape[0])]
        pltpu.make_async_copy(every, every, anchor_sem).wait()
        for copy in fold_copies():
            copy.wait()
        pltpu.make_async_copy(all_ref, all_ref, out_sem).wait()


def describe(
    chosen, source, folds, low, own, high, enc_w, enc_b, head_w, head_b, final_w, final_b
):
    rows, cols, chan = own.shape
    desc = final_w.shape[1]
    count = rows * cols // BLOCK
    whole = pl.BlockSpec(memory_space=pltpu.VMEM)
    scalars = pl.BlockSpec(memory_space=pltpu.SMEM)
    anywhere = pl.BlockSpec(memory_space=pl.ANY)
    macs = rows * cols * (12 * chan * chan + 9 * chan * desc + desc * desc)

    def half_lanes(n, height):
        return jax.ShapeDtypeStruct((n, height, LANES), jnp.bfloat16)

    return pl.pallas_call(
        describe_kernel,
        grid=(rows // ROWS_STEP,),
        in_specs=[scalars] * 2
        + [whole] * 3
        + [anywhere] * 4
        + [whole, anywhere, whole, anywhere, whole],
        out_specs=[pl.BlockSpec(memory_space=pl.ANY)] * 3,
        out_shape=[
            jax.ShapeDtypeStruct((count, BLOCK, desc), jnp.bfloat16),
            half_lanes(chosen.shape[0] // 2, 4 * BLOCK + FOLD_ROWS),
            half_lanes(source.shape[0] + 1, 2 * BLOCK),
        ],
        scratch_shapes=[
            pltpu.VMEM((rows + 4, cols, chan), jnp.bfloat16),
            pltpu.VMEM(enc_w.shape, jnp.bfloat16),
            pltpu.VMEM((9 * chan, desc), jnp.bfloat16),
            pltpu.VMEM(final_w.shape, jnp.bfloat16),
            pltpu.SemaphoreType.DMA((2 * (rows // ROWS_STEP),)),
            pltpu.SemaphoreType.DMA((3,)),
            pltpu.VMEM((rows + 4, cols, 3 * chan), jnp.bfloat16),
            pltpu.VMEM((rows + 2, cols, 3 * chan), jnp.bfloat16),
            pltpu.VMEM((12 * chan, 2 * chan), jnp.bfloat16),
            pltpu.VMEM((count, 2 * BLOCK, LANES), jnp.bfloat16),
            pltpu.VMEM((chosen.shape[0] // 2, FOLD_ROWS, LANES), jnp.bfloat16),
            pltpu.VMEM((source.shape[0], BLOCK), jnp.bfloat16),
            pltpu.SemaphoreType.DMA,
            pltpu.SemaphoreType.DMA,
            pltpu.SemaphoreType.DMA,
            pltpu.SemaphoreType.DMA((2,)),
        ],
        compiler_params=pltpu.CompilerParams(vmem_limit_bytes=56 * 2**20),
        cost_estimate=pl.CostEstimate(
            flops=2 * macs, bytes_accessed=rows * cols * (chan + desc) * 2, transcendentals=rows * cols
        ),
    )(
        chosen, source, chosen[None], source[None], folds, low, own, high, enc_w, enc_b[None], head_w.reshape(-1, desc),
        head_b[None], final_w, final_b[None],
    )


def match_kernel(
    slot_ref, anchors_ref, arrived_ref, out_ref, anchor_ref, partner_ref, anchor_fold_ref,
    partner_fold_ref, anchor_sem, partner_sem, fold_sem,
):
    groups = out_ref.shape[0] // PAIRS_STEP

    def products(left, right):
        return SCORE_SCALE * LOG2_E * lax.dot_general(
            left, right, (((1,), (1,)), ((), ())), preferred_element_type=jnp.float32
        )

    def relative_cost(folds):
        least = jnp.min(folds, axis=1, keepdims=True)
        return FOLD_PENALTY * LOG2_E * (folds - least)

    def group(g):
        return pl.ds(g * PAIRS_STEP, PAIRS_STEP)

    def anchors(g):
        return pltpu.make_async_copy(
            anchors_ref.at[group(g)], anchor_ref.at[group(g)], anchor_sem.at[g]
        )

    pairs = out_ref.shape[0]
    fold_copies = (
        pltpu.make_async_copy(
            arrived_ref.at[:, pl.ds(4 * BLOCK, FOLD_ROWS)], partner_fold_ref, fold_sem.at[0]
        ),
        pltpu.make_async_copy(
            anchors_ref.at[pairs, pl.ds(0, pairs)], anchor_fold_ref, fold_sem.at[1]
        ),
    )
    for copy in fold_copies:
        copy.start()

    def place(pair):
        return slot_ref[pair] // 2, pl.multiple_of(slot_ref[pair] % 2 * 2 * BLOCK, 2 * BLOCK)

    @pl.loop(0, groups)
    def _(g):
        anchors(g).start()
        for n in range(PAIRS_STEP):
            pair = g * PAIRS_STEP + n
            owner, start = place(pair)
            pltpu.make_async_copy(
                arrived_ref.at[owner, pl.ds(start, 2 * BLOCK)], partner_ref.at[pair], partner_sem.at[g]
            ).start()

    for copy in fold_copies:
        copy.wait()

    @pl.loop(0, groups)
    def _(g):
        anchor_cost = relative_cost(anchor_fold_ref[group(g)].astype(jnp.float32))
        anchor_column = jnp.transpose(anchor_cost)
        partner_fold = []
        for n in range(PAIRS_STEP):
            owner, start = place(g * PAIRS_STEP + n)
            both = partner_fold_ref[owner].astype(jnp.float32)
            partner_fold.append(jnp.where(start == 0, both[0:1], both[1:2]))
        partner_column = jnp.transpose(relative_cost(jnp.concatenate(partner_fold)))
        anchors(g).wait()
        here = partner_ref.at[group(g)]
        pltpu.make_async_copy(here, here, partner_sem.at[g]).wait()
        left, right = [
            [
                jnp.concatenate([ref[g * PAIRS_STEP + n, h * BLOCK : (h + 1) * BLOCK] for h in range(2)], axis=1)
                for n in range(PAIRS_STEP)
            ]
            for ref in (anchor_ref, partner_ref)
        ]

        over_i = []
        for n in range(PAIRS_STEP):
            by_i = products(left[n], right[n]) - anchor_column[:, n : n + 1]
            over_i.append(jnp.log2(jnp.sum(jnp.exp2(by_i), axis=0, keepdims=True)))
        over_i = jnp.transpose(jnp.concatenate(over_i))
        result = []
        for n in range(PAIRS_STEP):
            plain = products(right[n], left[n])
            by_j = plain - partner_column[:, n : n + 1]
            total = jnp.sum(jnp.exp2(by_j), axis=0, keepdims=True)
            best = jnp.max(by_j + (plain - over_i[:, n : n + 1]), axis=0, keepdims=True)
            result.append(jnp.exp2(best - anchor_cost[n : n + 1]) / total)
        out_ref[group(g)] = jnp.concatenate(result)


def match(slot, anchors, arrived):
    pairs = slot.shape[0]
    return pl.pallas_call(
        match_kernel,
        in_specs=[pl.BlockSpec(memory_space=pltpu.SMEM)] + [pl.BlockSpec(memory_space=pl.ANY)] * 2,
        out_specs=pl.BlockSpec(memory_space=pltpu.VMEM),
        out_shape=jax.ShapeDtypeStruct((pairs, BLOCK), jnp.float32),
        scratch_shapes=[pltpu.VMEM((pairs, 2 * BLOCK, LANES), jnp.bfloat16)] * 2
        + [
            pltpu.VMEM((pairs, BLOCK), jnp.bfloat16),
            pltpu.VMEM((arrived.shape[0], FOLD_ROWS, LANES), jnp.bfloat16),
        ]
        + [pltpu.SemaphoreType.DMA((pairs // PAIRS_STEP,))] * 2
        + [pltpu.SemaphoreType.DMA((2,))],
        compiler_params=pltpu.CompilerParams(vmem_limit_bytes=VMEM_MATCH),
    )(slot, anchors, arrived)


def local(
    features, fold_mask, encoder_weight, encoder_bias, head_weight, head_bias,
    final_weight, final_bias, pair_source, pair_target,
):
    own_band = features[0]
    band_rows, band_cols, _ = own_band.shape
    tile_count = lax.axis_size("tile")
    tile_here = lax.axis_index("tile")
    section = lax.axis_index("sec")
    swap = [(0, 1), (1, 0)]
    down = [(i, i + 1) for i in range(tile_count - 1)]
    up = [(j, i) for i, j in down]
    low = lax.ppermute(own_band[-2:], "tile", down)
    high = lax.ppermute(own_band[:2], "tile", up)

    block_count = band_rows * band_cols // BLOCK
    pair_count = pair_source.shape[1]
    capacity = 2
    wanted = lax.dynamic_index_in_dim(pair_target, 1 - section, 0, keepdims=False).reshape(
        tile_count, pair_count
    )
    matched = wanted // block_count == tile_here
    within = wanted % block_count
    lower = jnp.min(jnp.where(matched, within, block_count), axis=1)
    upper = jnp.max(jnp.where(matched, within, -1), axis=1)
    chosen = jnp.stack([jnp.where(upper >= 0, lower, -1), jnp.where(upper > lower, upper, -1)])
    targets = lax.dynamic_index_in_dim(wanted, tile_here, 0, keepdims=False)
    owners = targets // block_count
    lower_named = (owners[None, :] == owners[:, None]) & (targets[None, :] < targets[:, None])
    slot_rank = jnp.any(lower_named, axis=1).astype(jnp.int32)
    slot_index = owners * capacity + slot_rank

    described, send_blocks, anchors = describe(
        chosen.reshape(-1), pair_source[0], fold_mask[0], low, own_band, high, encoder_weight,
        encoder_bias, head_weight, head_bias, final_weight, final_bias,
    )
    sibling_anchors = lax.ppermute(anchors, "sec", swap)
    send_blocks, sibling_anchors, slot_index = lax.optimization_barrier(
        (send_blocks, sibling_anchors, slot_index)
    )
    arrived = lax.all_to_all(send_blocks, "tile", split_axis=0, concat_axis=0, tiled=True)
    confidence = match(slot_index, sibling_anchors, arrived)
    confidence = lax.ppermute(confidence, "sec", swap)
    return (described.reshape(1, band_rows, band_cols, -1), confidence[None])


def solution(mesh):
    return jax.shard_map(
        local,
        mesh=mesh,
        in_specs=(
            P("sec", "tile", None, None), P("sec", "tile", None), P(), P(), P(), P(), P(), P(),
            P("sec", "tile"), P(),
        ),
        out_specs=(P("sec", "tile", None, None), P("sec", "tile", None)),
        check_vma=False,
    )
```
